512 devices in a mesh: dp: 4 (over x), group: 16 (over y, z_lo), head: 8 (over z_hi, core).
Axes of the slice: x: 4, y: 8, z: 8 (z_hi: 4, z_lo: 2; z = z_hi * 2 + z_lo), core: 2. Of those that a mesh axis runs over, the one named last changes fastest.
Arguments:
- queries: bfloat16 [4, 16, 1024, 2048], P('dp', 'group', 'head'), may hold values from -130 to 130
- keys: bfloat16 [4, 16, 1024, 2048], P('dp', 'group', 'head'), may hold values from -4 to 4
- values: bfloat16 [4, 16, 1024, 2048], P('dp', 'group', 'head'), may hold values from -6 to 6
- noise: bfloat16 [4, 16, 1024, 3072], P('dp', 'group', 'head'), may hold values from -6 to 6
- projection: bfloat16 [2048, 3072], P('head', 'dp'), may hold values from -0.125 to 0.125
- rewards: float32 [4, 16], P('dp', 'group'), may hold values from -40 to 40
- counts: int32 [4], P('dp'), may hold values from 64 to 128, as said below
- step_index: int32 [1], replicated, may hold values from 1 to 49
Outputs:
- grad_queries: bfloat16 [4, 16, 1024, 2048], P('dp', 'group', 'head')
- grad_keys: bfloat16 [4, 16, 1024, 2048], P('dp', 'group', 'head')
- grad_values: bfloat16 [4, 16, 1024, 2048], P('dp', 'group', 'head')
- grad_projection: float32 [2048, 3072], P('head', 'dp')
The draws below stay inside these ranges and needn't reach their ends.
Inputs may be any that keep to these rules, and one draw needn't show every extreme that they name: `counts`: one prompt has 128 live text tokens and another 128 // 2.
All inputs are finite; a program needn't handle non-finite values.
Results may differ from the reference program's by a relative error of at most 0.014.
The reference program's roundings to bfloat16 on the way (of `dout`, `probs_low`, `output` and `dscores`) count: a program that leaves them out, or rounds other values in their place, can miss the bound.
Values may be sent and summed in bfloat16 or wider, within the bound.
A program may use at most 64 MiB of HBM per device.

```python
import jax
import jax.numpy as jnp
from jax import lax

D = 3072
HD = 128
TXT = 128
NSTEPS = 50
HW = 2048
SEQ = 1024
PROMPTS = 4
ROLLOUTS = 16


def key_normals(key):
    return jnp.clip(jax.random.normal(jax.random.fold_in(key, 101), (PROMPTS, ROLLOUTS, SEQ, HW), jnp.float32), -4.0, 4.0)


def draw_keys(key, part):
    base = key_normals(key)
    return base.astype(jnp.bfloat16)


def draw_queries(key, part):
    key = jax.random.fold_in(key, 5)
    queries = jnp.clip(jax.random.normal(key, (PROMPTS, ROLLOUTS, SEQ, HW), jnp.float32), -4.0, 4.0)
    return queries.astype(jnp.bfloat16)


def draw_rewards(key, part):
    key = jax.random.fold_in(key, 7)
    first, second, third = jax.random.split(key, 3)
    base = jnp.clip(jax.random.normal(first, (PROMPTS, 1), jnp.float32), -3.0, 3.0)
    gains = jax.random.uniform(second, (PROMPTS, 1), jnp.float32, 0.8, 1.2)
    spread = 0.05 * jnp.power(4.0, jnp.arange(PROMPTS, dtype=jnp.float32))[:, None] * gains
    ramp = 1.0 + 2.0 * jnp.arange(ROLLOUTS, dtype=jnp.float32)[None, :] / (ROLLOUTS - 1)
    noise_part = jnp.clip(jax.random.normal(third, (PROMPTS, ROLLOUTS), jnp.float32), -3.0, 3.0)
    return base + spread * ramp * noise_part


def draw_counts(key, part):
    key = jax.random.fold_in(key, 9)
    first, second = jax.random.split(key, 2)
    drawn = jax.random.randint(first, (PROMPTS,), TXT // 2, TXT + 1, dtype=jnp.int32)
    order = jax.random.permutation(second, PROMPTS)
    drawn = drawn.at[order[0]].set(TXT)
    drawn = drawn.at[order[1]].set(TXT // 2)
    return drawn


def spiked(values, own_key, source, target, shards_of, factor):
    owner, partner = [(jnp.arange(values.shape[dim]) // (values.shape[dim] // shards_of)).reshape([-1 if axis == dim else 1 for axis in range(values.ndim)]) for dim in (source, target)]
    chosen = jax.random.permutation(own_key, shards_of)[partner]
    strong = (owner == chosen) | (owner == (partner + shards_of // 2) % shards_of)
    return jnp.where(strong, factor * values, values)


def block_scale(own_key, extent, cuts, smallest, high):
    level, own = 1.0, jax.random.fold_in(own_key, 6)
    for dim, blocks in cuts:
        heights = jnp.exp(jax.random.uniform(jax.random.fold_in(own, dim), (blocks,), jnp.float32, smallest / len(cuts), high / len(cuts)))
        level = level * jnp.repeat(heights, extent[dim] // blocks).reshape([-1 if axis == dim else 1 for axis in range(len(extent))])
    return level


def normal_values(key, extent, deviation, limit, pieces=(), kind=jnp.bfloat16):
    level = block_scale(key, extent, pieces, -0.22, 0.18) if pieces else 1.0
    array = jax.random.normal(key, extent, jnp.float32) * deviation * level
    return jnp.minimum(jnp.maximum(array, -limit), limit).astype(kind)


def heavy_noise(own_key, shape, scale, most, pieces, heavy, held_as=jnp.bfloat16):
    result = scale * jax.random.normal(own_key, shape, jnp.float32)
    if pieces:
        result = result * block_scale(own_key, shape, pieces, -0.22, 0.18)
    return jnp.clip(spiked(result, jax.random.fold_in(own_key, 3), *heavy), -most, most).astype(held_as)


def setup_inputs(seed: int = 0) -> dict:
    key_list = jax.random.split(jax.random.key(seed), 9)
    queries = draw_queries(jax.random.fold_in(key_list[8], 71), 0)
    keys = draw_keys(jax.random.fold_in(key_list[8], 71), 0)
    values = normal_values(key_list[2], (PROMPTS, ROLLOUTS, SEQ, HW), 1.0, 6.0, ((0, 4), (1, 16), (2, 8)))
    noise = heavy_noise(key_list[3], (PROMPTS, ROLLOUTS, SEQ, D), 1.0, 6.0, ((0, 4), (1, 16), (2, 8)), (0, 3, 4, 2.0))
    projection = normal_values(key_list[4], (HW, D), HW ** -0.5, 0.125, ((0, 8), (1, 4)))
    rewards = draw_rewards(jax.random.fold_in(key_list[8], 71), 0)
    counts = draw_counts(jax.random.fold_in(key_list[8], 71), 0)
    step_index = jax.random.randint(key_list[7], (1,), 1, NSTEPS).astype(jnp.int32)
    return dict(queries=queries, keys=keys, values=values, noise=noise, projection=projection, rewards=rewards, counts=counts, step_index=step_index)


shift_factor = 7.0
noise_level = 0.7
loss_scale = 64.0
spread_floor = 0.25
masked_score = -1e+30

def step_factor(step_index):
    current = step_index[0].astype(jnp.float32)

    def level_at(position):
        remain = 1.0 - position / NSTEPS
        return shift_factor * remain / (1.0 + (shift_factor - 1.0) * remain)
    stride = level_at(current) - level_at(current + 1.0)
    return loss_scale * jnp.sqrt(stride) / (noise_level * ROLLOUTS)

def text_mask(live_text, length):
    position = jnp.arange(length, dtype=jnp.int32)
    return position < length - TXT + live_text

def head_grads(query_head, key_head, value_head, dout_head, usable):
    factor = HD ** (-0.5)
    scores = jnp.dot(query_head, key_head.T, preferred_element_type=jnp.float32) * factor
    scores = jnp.where(usable[None, :], scores, masked_score)
    row_peak = lax.optimization_barrier(jnp.max(scores, axis=1, keepdims=True))
    logsum = row_peak + jnp.log(lax.optimization_barrier(jnp.sum(jnp.exp(scores - row_peak), axis=1, keepdims=True)))
    attn_probs = jnp.exp(scores - logsum)
    probs_low = attn_probs.astype(jnp.bfloat16)
    output = jnp.dot(probs_low, value_head, preferred_element_type=jnp.float32).astype(jnp.bfloat16)
    row_dot = lax.optimization_barrier(jnp.sum(dout_head.astype(jnp.float32) * output.astype(jnp.float32), axis=1, keepdims=True))
    dprobs = jnp.dot(dout_head, value_head.T, preferred_element_type=jnp.float32)
    dscores = (attn_probs * (dprobs - row_dot)).astype(jnp.bfloat16)
    grad_query = jnp.dot(dscores, key_head, preferred_element_type=jnp.float32) * factor
    grad_key = jnp.dot(dscores.T, query_head, preferred_element_type=jnp.float32) * factor
    grad_value = jnp.dot(probs_low.T, dout_head, preferred_element_type=jnp.float32)
    return (output, grad_query, grad_key, grad_value)

def split_heads(matrix):
    return matrix.reshape(matrix.shape[0], -1, HD).transpose(1, 0, 2)

def join_heads(stack):
    return stack.transpose(1, 0, 2).reshape(stack.shape[1], -1)

def rollout_grads(query_rows, key_rows, value_rows, noise_rows, projection, usable, factor):
    dout = lax.dot_general(noise_rows, projection, (((1,), (1,)), ((), ())), preferred_element_type=jnp.float32).astype(jnp.bfloat16)

    def one_head(operands):
        return head_grads(operands[0], operands[1], operands[2], operands[3], usable)
    outputs, grad_query, grad_key, grad_value = lax.map(one_head, (split_heads(query_rows), split_heads(key_rows), split_heads(value_rows), split_heads(dout)))
    outputs = join_heads(outputs)
    weight_term = factor * lax.dot_general(noise_rows, outputs, (((0,), (0,)), ((), ())), preferred_element_type=jnp.float32)
    return ((factor * join_heads(grad_query)).astype(jnp.bfloat16), (factor * join_heads(grad_key)).astype(jnp.bfloat16), (factor * join_heads(grad_value)).astype(jnp.bfloat16), weight_term)

def mask_of(live_text):
    return text_mask(live_text, SEQ)

def reference(queries, keys, values, noise, projection, rewards, counts, step_index):
    base = step_factor(step_index)
    reward_avg = lax.optimization_barrier(jnp.mean(rewards, axis=1, keepdims=True))
    spread = jnp.sqrt(lax.optimization_barrier(jnp.mean((rewards - reward_avg) ** 2, axis=1, keepdims=True)))
    advantage = (rewards - reward_avg) / jnp.maximum(spread, spread_floor)
    factors = (base * advantage).reshape(-1)
    usable = jnp.repeat(jax.vmap(mask_of)(counts), ROLLOUTS, axis=0)
    total_rows = PROMPTS * ROLLOUTS

    def visit(summed, operands):
        grad_query, grad_key, grad_value, weight_term = rollout_grads(operands[0], operands[1], operands[2], operands[3], projection, operands[4], operands[5])
        return (summed + weight_term, (grad_query, grad_key, grad_value))
    summed, stacked = lax.scan(visit, jnp.zeros((D, HW), jnp.float32), (queries.reshape(total_rows, SEQ, HW), keys.reshape(total_rows, SEQ, HW), values.reshape(total_rows, SEQ, HW), noise.reshape(total_rows, SEQ, D), usable, factors))
    shape_out = (PROMPTS, ROLLOUTS, SEQ, HW)
    return (stacked[0].reshape(shape_out), stacked[1].reshape(shape_out), stacked[2].reshape(shape_out), summed.T)
```

```python
import functools
import math

import jax
import jax.numpy as jnp
from jax import lax
from jax.experimental import pallas as pl
from jax.experimental.pallas import tpu as pltpu
from jax.sharding import PartitionSpec as P

HD = 128
TXT = 128
NSTEPS = 50
SEQ = 1024
HW = 2048
D = 3072
HEADS = 8
DP = 4
GROUP = 16
TOK = SEQ // HEADS
FEAT = HW // HEADS
COLS = D // DP
CH = 256
NCH = SEQ // CH

shift_factor = 7.0
noise_level = 0.7
loss_scale = 64.0
spread_floor = 0.25
masked_score = -1e30

BF = jnp.bfloat16
F32 = jnp.float32
MESH = pl.DeviceIdType.MESH


def step_factor(step_index, rollout_count):
    current = step_index[0].astype(F32)

    def level_at(position):
        remain = 1.0 - position / NSTEPS
        return shift_factor * remain / (1.0 + (shift_factor - 1.0) * remain)

    stride = level_at(current) - level_at(current + 1.0)
    return loss_scale * jnp.sqrt(stride) / (noise_level * rollout_count)


def dot(a, b, ca, cb):
    return lax.dot_general(a, b, (((ca,), (cb,)), ((), ())), preferred_element_type=F32)


def kernel(
    q_in, k_in, v_in, n_in, p_in, rew_in, base_in, bias_in,
    gq_out, gk_out, gv_out, gp_out,
    qkv, nbuf, pbuf, rbuf, probs, kt, vt, out_t, dout_t, wacc, wlow, xrecv, grecv, glow, agbuf,
    grads, acc_k, acc_v,
    s_qkv, r_qkv, s_n, r_n, s_nf, r_nf, s_ns, r_ns, s_p, r_p, s_rew, r_rew,
    s_x, r_x, s_g, r_g, s_a, r_a, s_o, r_o,
):
    x = lax.axis_index("dp")
    g = lax.axis_index("group")
    me = lax.axis_index("head")
    core = lax.rem(me, 2)
    sib = me + 1 - 2 * core
    zup = lax.rem(me + 2, HEADS)
    zdn = lax.rem(me + HEADS - 2, HEADS)
    zop = lax.rem(me + 4, HEADS)

    def remote(src, dst, ssem, rsem, dev):
        return pltpu.make_async_remote_copy(
            src_ref=src, dst_ref=dst, send_sem=ssem, recv_sem=rsem, device_id=dev, device_id_type=MESH
        )

    def head_peer(r):
        return (x, g, lax.rem(me + r, HEADS))

    def dp_peer(r):
        return (lax.rem(x + r, DP), g, me)

    def group_peer(r):
        return (x, lax.rem(g + r, GROUP), me)

    def rows(block, size):
        return pl.ds(pl.multiple_of(block * size, size), size)

    barrier = pltpu.get_barrier_semaphore()

    def greet(count, peer):
        def body(r, carry):
            pl.semaphore_signal(barrier, inc=1, device_id=peer(r), device_id_type=MESH)
            return carry

        lax.fori_loop(1, count, body, 0)

    greet(HEADS, head_peer)
    greet(DP, dp_peer)
    greet(GROUP, group_peer)
    pl.semaphore_wait(barrier, HEADS + DP + GROUP - 3)

    mine = n_in.at[0, 0]
    own = nbuf.at[rows(me, TOK)]
    c_up = remote(mine, own, s_n.at[0], r_n.at[0], (x, g, zup))
    c_dn = remote(mine, own, s_n.at[1], r_n.at[1], (x, g, zdn))
    c_sib = remote(mine, own, s_ns.at[0], r_ns.at[0], (x, g, sib))
    c_own = pltpu.make_async_copy(mine, own, s_n.at[2])
    c_up.start()
    c_dn.start()
    c_sib.start()
    c_own.start()

    pcols = pl.ds(pl.multiple_of(x * COLS, COLS), COLS)

    def p_copy(r):
        return remote(p_in, pbuf.at[:, pcols], s_p.at[r], r_p.at[r], dp_peer(r))

    def rew_copy(r):
        return remote(rew_in, rbuf.at[r], s_rew.at[r], r_rew.at[r], group_peer(r))

    def start_all(count, make):
        def body(r, carry):
            make(r).start()
            return carry

        lax.fori_loop(1, count, body, 0)

    def wait_recv(count, make):
        def body(r, carry):
            make(r).wait_recv()
            return carry

        lax.fori_loop(1, count, body, 0)

    def wait_send(count, make):
        def body(r, carry):
            make(r).wait_send()
            return carry

        lax.fori_loop(1, count, body, 0)

    start_all(DP, p_copy)
    p_own = pltpu.make_async_copy(p_in, pbuf.at[:, pcols], s_p.at[0])
    p_own.start()

    ins = (q_in, k_in, v_in)

    def qkv_copy(a, h):
        def make(r):
            dst = lax.rem(me + r, HEADS)
            cols = pl.ds(pl.multiple_of(dst * FEAT + h * HD, HD), HD)
            return remote(
                ins[a].at[0, 0, :, cols], qkv.at[a, h, rows(me, TOK)],
                s_qkv.at[a, h, r], r_qkv.at[a, h, r], (x, g, dst),
            )

        return make

    def qkv_own(a, h):
        cols = pl.ds(pl.multiple_of(me * FEAT + h * HD, HD), HD)
        return pltpu.make_async_copy(
            ins[a].at[0, 0, :, cols], qkv.at[a, h, rows(me, TOK)], s_qkv.at[a, h, 0]
        )

    for h in range(2):
        for a in range(3):
            start_all(HEADS, qkv_copy(a, h))
            qkv_own(a, h).start()
    start_all(GROUP, rew_copy)

    wait_recv(GROUP, rew_copy)
    rbuf[0] = rew_in[...]
    rewards = rbuf[...]
    average = jnp.sum(rewards, axis=0) / GROUP
    variance = jnp.sum((rewards - average[None]) ** 2, axis=0) / GROUP
    factor = base_in[...] * ((rew_in[...] - average) / jnp.maximum(jnp.sqrt(variance), spread_floor))
    factor = factor[0:1, :]

    def forward(sem, source, half, target):
        part = nbuf.at[pl.ds(pl.multiple_of(source * TOK + half * (TOK // 2), TOK // 2), TOK // 2)]
        return remote(part, part, s_nf.at[sem], r_nf.at[sem], (x, g, target))

    def to_sib(slot, source):
        part = nbuf.at[rows(source, TOK)]
        return remote(part, part, s_ns.at[slot], r_ns.at[slot], (x, g, sib))

    f_up = forward(0, zdn, 0, zup)
    f_dn = forward(1, zup, 1, zdn)
    sib_dn = to_sib(1, zdn)
    sib_up = to_sib(2, zup)
    sib_op = to_sib(3, zop)
    c_up.wait_recv()
    f_up.start()
    sib_dn.start()
    c_dn.wait_recv()
    f_dn.start()
    sib_up.start()

    p_own.wait()
    wait_recv(DP, p_copy)

    def make_dout(block):
        tokens = rows(block // 2, CH)
        part = dot(pbuf[...], nbuf[tokens, :], 1, 1)
        dout_t[block // 2] = part.astype(BF)

    def add_weight(block, first):
        pair = block // 2
        lhs = out_t[pair]

        def body(j, carry):
            cols = pl.ds(pl.multiple_of(j * COLS, COLS), COLS)
            part = dot(lhs, nbuf[rows(pair, CH), cols], 1, 0)
            if first:
                wacc[j] = part
            else:
                wacc[j] += part
            return carry

        lax.fori_loop(0, DP, body, 0)

    c_own.wait()
    c_sib.wait_recv()
    make_dout(me)
    sib_dn.wait_recv()
    make_dout(zdn)
    sib_up.wait_recv()
    make_dout(zup)

    scale = HD ** (-0.5)

    def forward_head(h):
        for a in range(3):
            qkv_own(a, h).wait()
            wait_recv(HEADS, qkv_copy(a, h))
        kt[h] = qkv[1, h].T
        vt[h] = qkv[2, h].T

        def body(c, carry):
            qc = qkv[0, h, rows(c, CH), :]
            t = dot(qkv[1, h], qc, 1, 1) * (scale * math.log2(math.e))
            t = jnp.concatenate([t[: SEQ - TXT], t[SEQ - TXT :] + bias_in[...]], axis=0)
            peak = jnp.max(t, axis=0, keepdims=True)
            e = jnp.exp2(t - peak)
            total = jnp.sum(e, axis=0, keepdims=True)
            pr = e * (1.0 / total)
            probs[h, c] = pr
            part = dot(vt[h], pr.astype(BF), 1, 0)
            out_t[c, pl.ds(h * HD, HD), :] = part.astype(BF)
            return carry

        lax.fori_loop(0, NCH, body, 0)

    forward_head(0)
    forward_head(1)
    add_weight(me, True)
    add_weight(zdn, False)
    add_weight(zup, False)

    f_up.wait_recv()
    f_dn.wait_recv()
    sib_op.start()
    sib_op.wait_recv()
    make_dout(zop)
    add_weight(zop, False)
    for j in range(DP):
        wlow[j] = (wacc[j] * factor[0:1, 0:1]).astype(BF)

    def x_copy(r):
        return remote(wlow.at[lax.rem(x + r, DP)], xrecv.at[r], s_x.at[r], r_x.at[r], dp_peer(r))

    start_all(DP, x_copy)

    outs = (gq_out, gk_out, gv_out)

    def out_copy(a, h):
        cols = pl.ds(pl.multiple_of(me * FEAT + h * HD, HD), HD)

        def make(r):
            dst = lax.rem(me + r, HEADS)
            return remote(
                grads.at[a, h, rows(dst, TOK)], outs[a].at[0, 0, :, cols],
                s_o.at[a, h, r], r_o.at[a, h, r], (x, g, dst),
            )

        return make

    def out_own(a, h):
        cols = pl.ds(pl.multiple_of(me * FEAT + h * HD, HD), HD)
        return pltpu.make_async_copy(
            grads.at[a, h, rows(me, TOK)], outs[a].at[0, 0, :, cols], s_o.at[a, h, 0]
        )

    def backward_head(h):
        acc_k[...] = jnp.zeros_like(acc_k)
        acc_v[...] = jnp.zeros_like(acc_v)

        def body(c, carry):
            pr = probs[h, c]
            dt = dout_t[c, pl.ds(h * HD, HD), :]
            ot = out_t[c, pl.ds(h * HD, HD), :]
            row_dot = jnp.sum(dt.astype(F32) * ot.astype(F32), axis=0, keepdims=True)
            dp = dot(qkv[2, h], dt, 1, 0)
            ds = (pr * (dp - row_dot)).astype(BF)
            gqt = dot(kt[h], ds, 1, 0)
            grads[0, h, rows(c, CH), :] = (gqt.T * (scale * factor)).astype(BF)
            acc_k[...] += dot(ds, qkv[0, h, rows(c, CH), :], 1, 0)
            acc_v[...] += dot(pr.astype(BF), dt, 1, 1)
            return carry

        lax.fori_loop(0, NCH, body, 0)
        grads[1, h] = (acc_k[...] * (scale * factor)).astype(BF)
        grads[2, h] = (acc_v[...] * factor).astype(BF)
        for a in range(3):
            start_all(HEADS, out_copy(a, h))
            out_own(a, h).start()

    backward_head(0)
    backward_head(1)

    wait_recv(DP, x_copy)
    total = wlow[x].astype(F32)
    for r in range(1, DP):
        total = total + xrecv[r].astype(F32)
    glow[...] = total.reshape(GROUP, 16, COLS).astype(BF)

    def g_copy(r):
        return remote(glow.at[lax.rem(g + r, GROUP)], grecv.at[r], s_g.at[r], r_g.at[r], group_peer(r))

    start_all(GROUP, g_copy)
    wait_recv(GROUP, g_copy)
    part = glow[g].astype(F32)
    for r in range(1, GROUP):
        part = part + grecv[r].astype(F32)
    agbuf[g] = part.astype(BF)

    def a_copy(r):
        return remote(agbuf.at[g], agbuf.at[g], s_a.at[r], r_a.at[r], group_peer(r))

    start_all(GROUP, a_copy)
    wait_recv(GROUP, a_copy)
    gp_out[...] = agbuf[...].astype(F32).reshape(FEAT, COLS)

    for h in range(2):
        for a in range(3):
            wait_recv(HEADS, out_copy(a, h))
            out_own(a, h).wait()
            wait_send(HEADS, out_copy(a, h))
            wait_send(HEADS, qkv_copy(a, h))
    wait_send(GROUP, a_copy)
    wait_send(GROUP, g_copy)
    wait_send(DP, x_copy)
    wait_send(DP, p_copy)
    wait_send(GROUP, rew_copy)
    for c in (c_up, c_dn, c_sib, f_up, f_dn, sib_dn, sib_up, sib_op):
        c.wait_send()


def local(queries, keys, values, noise, projection, rewards, counts, step_index):
    base = jnp.full((8, 128), step_factor(step_index, GROUP), F32)
    rew = jnp.full((8, 128), rewards[0, 0], F32)
    slot = jnp.arange(TXT, dtype=jnp.int32)
    bias = jnp.broadcast_to(jnp.where(slot < counts[0], 0.0, masked_score).astype(F32)[:, None], (TXT, CH))
    grad = jax.ShapeDtypeStruct((1, 1, TOK, HW), BF)
    hbm = pl.BlockSpec(memory_space=pl.ANY)
    vmem = pl.BlockSpec(memory_space=pltpu.VMEM)
    dma = pltpu.SemaphoreType.DMA
    return pl.pallas_call(
        kernel,
        out_shape=(grad, grad, grad, jax.ShapeDtypeStruct((FEAT, COLS), F32)),
        in_specs=[hbm] * 5 + [vmem] * 3,
        out_specs=(hbm, hbm, hbm, vmem),
        scratch_shapes=[
            pltpu.VMEM((3, 2, SEQ, HD), BF),
            pltpu.VMEM((SEQ, D), BF),
            pltpu.VMEM((FEAT, D), BF),
            pltpu.VMEM((GROUP, 8, 128), F32),
            pltpu.VMEM((2, NCH, SEQ, CH), F32),
            pltpu.VMEM((2, HD, SEQ), BF),
            pltpu.VMEM((2, HD, SEQ), BF),
            pltpu.VMEM((NCH, FEAT, CH), BF),
            pltpu.VMEM((NCH, FEAT, CH), BF),
            pltpu.VMEM((DP, FEAT, COLS), F32),
            pltpu.VMEM((DP, FEAT, COLS), BF),
            pltpu.VMEM((DP, FEAT, COLS), BF),
            pltpu.VMEM((GROUP, 16, COLS), BF),
            pltpu.VMEM((GROUP, 16, COLS), BF),
            pltpu.VMEM((GROUP, 16, COLS), BF),
            pltpu.VMEM((3, 2, SEQ, HD), BF),
            pltpu.VMEM((SEQ, HD), F32),
            pltpu.VMEM((SEQ, HD), F32),
            dma((3, 2, HEADS)), dma((3, 2, HEADS)),
            dma((3,)), dma((3,)),
            dma((2,)), dma((2,)),
            dma((4,)), dma((4,)),
            dma((DP,)), dma((DP,)),
            dma((GROUP,)), dma((GROUP,)),
            dma((DP,)), dma((DP,)),
            dma((GROUP,)), dma((GROUP,)),
            dma((GROUP,)), dma((GROUP,)),
            dma((3, 2, HEADS)), dma((3, 2, HEADS)),
        ],
        compiler_params=pltpu.CompilerParams(
            collective_id=0, has_side_effects=True, vmem_limit_bytes=58 << 20
        ),
        name="rollout_grads",
    )(queries, keys, values, noise, projection, rew, base, bias)


def solution(mesh):
    in_specs = (
        P("dp", "group", "head", None),
        P("dp", "group", "head", None),
        P("dp", "group", "head", None),
        P("dp", "group", "head", None),
        P("head", "dp"),
        P("dp", "group"),
        P("dp"),
        P(),
    )
    out_specs = (
        P("dp", "group", "head", None),
        P("dp", "group", "head", None),
        P("dp", "group", "head", None),
        P("head", "dp"),
    )
    return jax.shard_map(local, mesh=mesh, in_specs=in_specs, out_specs=out_specs, check_vma=False)
```

```python
import functools
import math

import jax
import jax.numpy as jnp
from jax import lax
from jax.experimental import pallas as pl
from jax.experimental.pallas import tpu as pltpu
from jax.sharding import PartitionSpec as P

HD = 128
TXT = 128
NSTEPS = 50
SEQ = 1024
HW = 2048
D = 3072
HEADS = 8
DP = 4
GROUP = 16
TOK = SEQ // HEADS
FEAT = HW // HEADS
COLS = D // DP
CH = 256
NCH = SEQ // CH

shift_factor = 7.0
noise_level = 0.7
loss_scale = 64.0
spread_floor = 0.25
masked_score = -1e30

BF = jnp.bfloat16
F32 = jnp.float32
MESH = pl.DeviceIdType.MESH


def step_factor(step_index, rollout_count):
    current = step_index[0].astype(F32)

    def level_at(position):
        remain = 1.0 - position / NSTEPS
        return shift_factor * remain / (1.0 + (shift_factor - 1.0) * remain)

    stride = level_at(current) - level_at(current + 1.0)
    return loss_scale * jnp.sqrt(stride) / (noise_level * rollout_count)


def dot(a, b, ca, cb):
    return lax.dot_general(a, b, (((ca,), (cb,)), ((), ())), preferred_element_type=F32)


def kernel(
    q_in, k_in, v_in, n_in, p_in, rew_in, base_in, bias_in,
    gq_out, gk_out, gv_out, gp_out,
    qkv, nx, pcol, rbuf, fbuf, probs, kt, vt, out_t, part_s, part_own, part_r, dout_s, dout_t, oz, ox, wlow, yrecv, zlow, zrecv, agbuf,
    grads, acc_k, acc_v,
    s_qkv, r_qkv, s_nx, r_nx, s_ns, r_ns, s_p1, r_p1, s_up, r_up, s_dn, r_dn, s_pt, r_pt,
    s_rew, r_rew, s_f, r_f, s_d, r_d, s_out, r_out, s_x, r_x, s_y, r_y, s_z, r_z, s_a, r_a, s_o, r_o,
):
    x = lax.axis_index("dp")
    g = lax.axis_index("group")
    me = lax.axis_index("head")
    y = g // 2
    zlo = lax.rem(g, 2)
    zhi = me // 2
    core = lax.rem(me, 2)
    sib = me + 1 - 2 * core

    def remote(src, dst, ssem, rsem, dev):
        return pltpu.make_async_remote_copy(
            src_ref=src, dst_ref=dst, send_sem=ssem, recv_sem=rsem, device_id=dev, device_id_type=MESH
        )

    def head_peer(r):
        return (x, g, lax.rem(me + r, HEADS))

    def zhi_peer(r):
        return (x, g, lax.rem(me + 2 * r, HEADS))

    def dp_peer(r):
        return (lax.rem(x + r, DP), g, me)

    def group_peer(r):
        return (x, lax.rem(g + r, GROUP), me)

    def y_peer(r):
        return (x, lax.rem(g + 2 * r, GROUP), me)

    def z_place(r):
        return lax.rem(2 * zhi + zlo + r, 8)

    def z_peer(r):
        place = z_place(r)
        return (x, 2 * y + lax.rem(place, 2), 2 * (place // 2) + core)

    def rows(block, size):
        return pl.ds(pl.multiple_of(block * size, size), size)

    def each(count, make, *acts):
        def body(r, carry):
            copy = make(r)
            for act in acts:
                getattr(copy, act)()
            return carry

        lax.fori_loop(1, count, body, 0)

    barrier = pltpu.get_barrier_semaphore()

    def greet(count, peer):
        def body(r, carry):
            pl.semaphore_signal(barrier, inc=1, device_id=peer(r), device_id_type=MESH)
            return carry

        lax.fori_loop(1, count, body, 0)

    greet(HEADS, head_peer)
    greet(DP, dp_peer)
    greet(GROUP, group_peer)

    def far_peer(r):
        return (x, g + 1 - 2 * zlo, lax.rem(me + 2 * r, HEADS))

    greet(4, far_peer)
    pl.semaphore_wait(barrier, HEADS + DP + GROUP + 4 - 4)

    xcols = pl.ds(pl.multiple_of(x * COLS, COLS), COLS)

    def p1_copy(r):
        return remote(p_in.at[y], pcol.at[y, zhi], s_p1.at[r], r_p1.at[r], zhi_peer(r))

    each(4, p1_copy, "start")
    p_own = pltpu.make_async_copy(p_in, pcol.at[:, zhi], s_p1.at[0])
    p_own.start()

    def nx_copy(r):
        dst = lax.rem(x + r, DP)
        cols = pl.ds(pl.multiple_of(dst * COLS, COLS), COLS)
        return remote(
            n_in.at[0, 0, :, cols], nx.at[x, rows(core, TOK)], s_nx.at[r], r_nx.at[r], (dst, g, me)
        )

    each(DP, nx_copy, "start")
    nx_own = pltpu.make_async_copy(n_in.at[0, 0, :, xcols], nx.at[x, rows(core, TOK)], s_nx.at[0])
    nx_own.start()

    def rew_copy(r):
        return remote(rew_in, rbuf.at[r], s_rew.at[r], r_rew.at[r], group_peer(r))

    each(GROUP, rew_copy, "start")

    ins = (q_in, k_in, v_in)

    def qkv_copy(a, h):
        def make(r):
            dst = lax.rem(me + r, HEADS)
            cols = pl.ds(pl.multiple_of(dst * FEAT + h * HD, HD), HD)
            return remote(
                ins[a].at[0, 0, :, cols], qkv.at[a, h, rows(me, TOK)],
                s_qkv.at[a, h, r], r_qkv.at[a, h, r], (x, g, dst),
            )

        return make

    def qkv_own(a, h):
        cols = pl.ds(pl.multiple_of(me * FEAT + h * HD, HD), HD)
        return pltpu.make_async_copy(
            ins[a].at[0, 0, :, cols], qkv.at[a, h, rows(me, TOK)], s_qkv.at[a, h, 0]
        )

    def start_head(h):
        for a in range(3):
            each(HEADS, qkv_copy(a, h), "start")
            qkv_own(a, h).start()

    def ring_up(d, j):
        part = pcol.at[lax.rem(y + 8 - d, 8), lax.rem(zhi + 1 + j, 4)]
        return remote(part, part, s_up.at[d, j], r_up.at[d, j], y_peer(1))

    def ring_dn(d, j):
        part = pcol.at[lax.rem(y + d, 8), lax.rem(zhi + 1 + j, 4)]
        return remote(part, part, s_dn.at[d, j], r_dn.at[d, j], y_peer(7))

    def up_hop(d, j):
        return d < 3 or (d == 3 and j < 2)

    def dn_hop(d, j):
        return d < 3 or (d == 3 and j == 2)

    each(4, p1_copy, "wait_recv")
    for j in range(3):
        ring_up(0, j).start()
        ring_dn(0, j).start()
    start_head(0)

    each(GROUP, rew_copy, "wait_recv")
    rbuf[0] = rew_in[...]
    rewards = rbuf[...]
    average = jnp.sum(rewards, axis=0) / GROUP
    variance = jnp.sum((rewards - average[None]) ** 2, axis=0) / GROUP
    fbuf[x] = base_in[...] * ((rew_in[...] - average) / jnp.maximum(jnp.sqrt(variance), spread_floor))

    def f_copy(r):
        return remote(fbuf.at[x], fbuf.at[x], s_f.at[r], r_f.at[r], dp_peer(r))

    each(DP, f_copy, "start")
    factor = fbuf[x][0:1, :]

    each(DP, nx_copy, "wait_recv")
    nx_own.wait()
    nx_part = nx.at[:, rows(core, TOK)]
    nx_sib = remote(nx_part, nx_part, s_ns.at[0], r_ns.at[0], (x, g, sib))
    nx_sib.start()

    p_own.wait()

    def part_copy(b):
        def make(r):
            dst = lax.rem(x + r, DP)
            return remote(
                part_s.at[dst, :, rows(b, 32)], part_r.at[r, :, rows(b, 32)],
                s_pt.at[b, r], r_pt.at[b, r], (dst, g, me),
            )

        return make

    def make_part(blocks):
        lhs = jnp.concatenate([pcol[b].reshape(4 * 32, COLS) for b in blocks], axis=0)

        def body(r, carry):
            k = lax.rem(x + r, DP)
            part = dot(lhs, nx[k], 1, 1)
            low = part.astype(BF)
            for i, b in enumerate(blocks):
                for z in range(4):
                    part_s[k, z, rows(b, 32), :] = low[i * 128 + z * 32 : i * 128 + (z + 1) * 32]
            return carry

        lax.fori_loop(1, DP, body, 0)
        part = dot(lhs, nx[x], 1, 1)
        for i, b in enumerate(blocks):
            for z in range(4):
                part_own[z, rows(b, 32), :] = part[i * 128 + z * 32 : i * 128 + (z + 1) * 32]
        for b in blocks:
            each(DP, part_copy(b), "start")

    def sum_parts():
        def body(b, carry):
            each(DP, part_copy(b), "wait_recv")
            return carry

        lax.fori_loop(0, 8, body, 0)
        for z in range(4):
            total = part_own[z]
            for r in range(1, DP):
                total = total + part_r[r, z].astype(F32)
            dout_s[z] = total.astype(BF)

    scale = HD ** (-0.5)

    def out_copy(h):
        def make(r):
            dst = lax.rem(zhi + r, 4)
            return remote(
                out_t.at[dst, pl.ds(h * HD, HD)], oz.at[zhi, pl.ds(h * HD, HD)],
                s_out.at[h, r], r_out.at[h, r], zhi_peer(r),
            )

        return make

    def out_own(h):
        return pltpu.make_async_copy(
            out_t.at[zhi, pl.ds(h * HD, HD)], oz.at[zhi, pl.ds(h * HD, HD)], s_out.at[h, 0]
        )

    def forward_head(h):
        for a in range(3):
            qkv_own(a, h).wait()
            each(HEADS, qkv_copy(a, h), "wait_recv")
        kt[h] = qkv[1, h].T
        vt[h] = qkv[2, h].T

        def body(c, carry):
            qc = qkv[0, h, rows(c, CH), :]
            t = dot(qkv[1, h], qc, 1, 1) * (scale * math.log2(math.e))
            t = jnp.concatenate([t[: SEQ - TXT], t[SEQ - TXT :] + bias_in[...]], axis=0)
            peak = jnp.max(t, axis=0, keepdims=True)
            e = jnp.exp2(t - peak)
            total = jnp.sum(e, axis=0, keepdims=True)
            pr = e * (1.0 / total)
            probs[h, c] = pr
            part = dot(vt[h], pr.astype(BF), 1, 0)
            out_t[c, pl.ds(h * HD, HD), :] = part.astype(BF)
            return carry

        lax.fori_loop(0, NCH, body, 0)
        each(4, out_copy(h), "start")
        out_own(h).start()

    def ring_step(d):
        for j in range(3):
            if up_hop(d - 1, j):
                ring_up(d - 1, j).wait_recv()
                if up_hop(d, j):
                    ring_up(d, j).start()
            if dn_hop(d - 1, j):
                ring_dn(d - 1, j).wait_recv()
                if dn_hop(d, j):
                    ring_dn(d, j).start()

    def x_copy(h):
        part = oz.at[:, pl.ds(h * HD, HD)]

        def make(r):
            return remote(part, ox.at[x, :, pl.ds(h * HD, HD)], s_x.at[h, r], r_x.at[h, r], dp_peer(r))

        return make

    def x_own(h):
        return pltpu.make_async_copy(
            oz.at[:, pl.ds(h * HD, HD)], ox.at[x, :, pl.ds(h * HD, HD)], s_x.at[h, 0]
        )

    def share_out(h):
        out_own(h).wait()
        each(4, out_copy(h), "wait_recv")
        each(DP, x_copy(h), "start")
        x_own(h).start()

    def y_copy(h):
        def make(r):
            dst = lax.rem(y + r, 8)
            return remote(
                wlow.at[h, :, rows(dst, 16)], yrecv.at[h, r], s_y.at[h, r], r_y.at[h, r], y_peer(r)
            )

        return make

    def weight(h):
        x_own(h).wait()
        each(DP, x_copy(h), "wait_recv")

        def body(z, carry):
            total = jnp.zeros((HD, COLS), F32)
            for k in range(DP):
                part = dot(ox[k, z, pl.ds(h * HD, HD), :], nx[k], 1, 0)
                total = total + part * fbuf[k][0:1, 0:1]
            wlow[h, z] = total.astype(BF)
            return carry

        lax.fori_loop(0, 4, body, 0)
        each(8, y_copy(h), "start")

    nx_sib.wait_recv()
    make_part([y])
    ring_step(1)
    make_part([lax.rem(y + 7, 8), lax.rem(y + 1, 8)])
    ring_step(2)
    make_part([lax.rem(y + 6, 8), lax.rem(y + 2, 8)])
    ring_step(3)
    make_part([lax.rem(y + 5, 8), lax.rem(y + 3, 8)])
    ring_step(4)
    make_part([lax.rem(y + 4, 8)])

    def d_copy(r):
        dst = lax.rem(zhi + r, 4)
        return remote(dout_s.at[dst], dout_t.at[zhi], s_d.at[r], r_d.at[r], zhi_peer(r))

    start_head(1)
    forward_head(0)
    sum_parts()
    each(4, d_copy, "start")
    d_own = pltpu.make_async_copy(dout_s.at[zhi], dout_t.at[zhi], s_d.at[0])
    d_own.start()
    share_out(0)
    forward_head(1)
    each(DP, f_copy, "wait_recv")
    weight(0)
    share_out(1)

    outs = (gq_out, gk_out, gv_out)

    def grad_copy(a, h):
        cols = pl.ds(pl.multiple_of(me * FEAT + h * HD, HD), HD)

        def make(r):
            dst = lax.rem(me + r, HEADS)
            return remote(
                grads.at[a, h, rows(dst, TOK)], outs[a].at[0, 0, :, cols],
                s_o.at[a, h, r], r_o.at[a, h, r], (x, g, dst),
            )

        return make

    def grad_own(a, h):
        cols = pl.ds(pl.multiple_of(me * FEAT + h * HD, HD), HD)
        return pltpu.make_async_copy(
            grads.at[a, h, rows(me, TOK)], outs[a].at[0, 0, :, cols], s_o.at[a, h, 0]
        )

    def backward_head(h):
        acc_k[...] = jnp.zeros_like(acc_k)
        acc_v[...] = jnp.zeros_like(acc_v)

        def body(c, carry):
            pr = probs[h, c]
            dt = dout_t[c, pl.ds(h * HD, HD), :]
            ot = out_t[c, pl.ds(h * HD, HD), :]
            row_dot = jnp.sum(dt.astype(F32) * ot.astype(F32), axis=0, keepdims=True)
            dp = dot(qkv[2, h], dt, 1, 0)
            ds = (pr * (dp - row_dot)).astype(BF)
            gqt = dot(kt[h], ds, 1, 0)
            grads[0, h, rows(c, CH), :] = (gqt.T * (scale * factor)).astype(BF)
            acc_k[...] += dot(ds, qkv[0, h, rows(c, CH), :], 1, 0)
            acc_v[...] += dot(pr.astype(BF), dt, 1, 1)
            return carry

        lax.fori_loop(0, NCH, body, 0)
        grads[1, h] = (acc_k[...] * (scale * factor)).astype(BF)
        grads[2, h] = (acc_v[...] * factor).astype(BF)
        for a in range(3):
            each(HEADS, grad_copy(a, h), "start")
            grad_own(a, h).start()

    d_own.wait()
    each(4, d_copy, "wait_recv")
    backward_head(0)
    backward_head(1)
    weight(1)

    for h in range(2):
        each(8, y_copy(h), "wait_recv")
        total = wlow[h, :, rows(y, 16), :].astype(F32)
        for r in range(1, 8):
            total = total + yrecv[h, r].astype(F32)
        for z in range(4):
            zlow[2 * z + h] = total[z].astype(BF)

    def z_copy(r):
        return remote(zlow.at[z_place(r)], zrecv.at[r], s_z.at[r], r_z.at[r], z_peer(r))

    each(8, z_copy, "start")
    each(8, z_copy, "wait_recv")
    part = zlow[2 * zhi + zlo].astype(F32)
    for r in range(1, 8):
        part = part + zrecv[r].astype(F32)
    place = zlo * 8 + y
    agbuf[place] = part.astype(BF)

    def a_copy(r):
        return remote(agbuf.at[place], agbuf.at[place], s_a.at[r], r_a.at[r], group_peer(r))

    each(GROUP, a_copy, "start")
    each(GROUP, a_copy, "wait_recv")
    gp_out[...] = agbuf[...].astype(F32).reshape(FEAT, COLS)

    for h in range(2):
        for a in range(3):
            grad_own(a, h).wait()
            each(HEADS, grad_copy(a, h), "wait_recv", "wait_send")
            each(HEADS, qkv_copy(a, h), "wait_send")
        each(4, out_copy(h), "wait_send")
        each(DP, x_copy(h), "wait_send")
        each(8, y_copy(h), "wait_send")
    for j in range(3):
        for d in range(4):
            if up_hop(d, j):
                ring_up(d, j).wait_send()
            if dn_hop(d, j):
                ring_dn(d, j).wait_send()
    each(4, p1_copy, "wait_send")
    each(DP, nx_copy, "wait_send")
    each(DP, f_copy, "wait_send")
    each(GROUP, rew_copy, "wait_send")
    each(4, d_copy, "wait_send")
    each(8, z_copy, "wait_send")
    each(GROUP, a_copy, "wait_send")
    for b in range(8):
        each(DP, part_copy(b), "wait_send")
    nx_sib.wait_send()


def local(queries, keys, values, noise, projection, rewards, counts, step_index):
    base = jnp.full((8, 128), step_factor(step_index, GROUP), F32)
    rew = jnp.full((8, 128), rewards[0, 0], F32)
    slot = jnp.arange(TXT, dtype=jnp.int32)
    bias = jnp.broadcast_to(jnp.where(slot < counts[0], 0.0, masked_score).astype(F32)[:, None], (TXT, CH))
    grad = jax.ShapeDtypeStruct((1, 1, TOK, HW), BF)
    hbm = pl.BlockSpec(memory_space=pl.ANY)
    vmem = pl.BlockSpec(memory_space=pltpu.VMEM)
    dma = pltpu.SemaphoreType.DMA
    return pl.pallas_call(
        kernel,
        out_shape=(grad, grad, grad, jax.ShapeDtypeStruct((FEAT, COLS), F32)),
        in_specs=[hbm] * 5 + [vmem] * 3,
        out_specs=(hbm, hbm, hbm, vmem),
        scratch_shapes=[
            pltpu.VMEM((3, 2, SEQ, HD), BF),
            pltpu.VMEM((DP, 2 * TOK, COLS), BF),
            pltpu.VMEM((8, 4, 32, COLS), BF),
            pltpu.VMEM((GROUP, 8, 128), F32),
            pltpu.VMEM((DP, 8, 128), F32),
            pltpu.VMEM((2, NCH, SEQ, CH), F32),
            pltpu.VMEM((2, HD, SEQ), BF),
            pltpu.VMEM((2, HD, SEQ), BF),
            pltpu.VMEM((NCH, FEAT, CH), BF),
            pltpu.VMEM((DP, NCH, FEAT, CH), BF),
            pltpu.VMEM((NCH, FEAT, CH), F32),
            pltpu.VMEM((DP, NCH, FEAT, CH), BF),
            pltpu.VMEM((NCH, FEAT, CH), BF),
            pltpu.VMEM((NCH, FEAT, CH), BF),
            pltpu.VMEM((NCH, FEAT, CH), BF),
            pltpu.VMEM((DP, NCH, FEAT, CH), BF),
            pltpu.VMEM((2, 4, HD, COLS), BF),
            pltpu.VMEM((2, 8, 4, 16, COLS), BF),
            pltpu.VMEM((8, 16, COLS), BF),
            pltpu.VMEM((8, 16, COLS), BF),
            pltpu.VMEM((GROUP, 16, COLS), BF),
            pltpu.VMEM((3, 2, SEQ, HD), BF),
            pltpu.VMEM((SEQ, HD), F32),
            pltpu.VMEM((SEQ, HD), F32),
            dma((3, 2, HEADS)), dma((3, 2, HEADS)),
            dma((DP,)), dma((DP,)),
            dma((1,)), dma((1,)),
            dma((4,)), dma((4,)),
            dma((4, 3)), dma((4, 3)),
            dma((4, 3)), dma((4, 3)),
            dma((8, DP)), dma((8, DP)),
            dma((GROUP,)), dma((GROUP,)),
            dma((DP,)), dma((DP,)),
            dma((4,)), dma((4,)),
            dma((2, 4)), dma((2, 4)),
            dma((2, DP)), dma((2, DP)),
            dma((2, 8)), dma((2, 8)),
            dma((8,)), dma((8,)),
            dma((GROUP,)), dma((GROUP,)),
            dma((3, 2, HEADS)), dma((3, 2, HEADS)),
        ],
        compiler_params=pltpu.CompilerParams(
            collective_id=0, has_side_effects=True, vmem_limit_bytes=58 << 20
        ),
        name="rollout_grads",
    )(queries, keys, values, noise, projection.reshape(8, 32, COLS), rew, base, bias)


def solution(mesh):
    in_specs = (
        P("dp", "group", "head", None),
        P("dp", "group", "head", None),
        P("dp", "group", "head", None),
        P("dp", "group", "head", None),
        P("head", "dp"),
        P("dp", "group"),
        P("dp"),
        P(),
    )
    out_specs = (
        P("dp", "group", "head", None),
        P("dp", "group", "head", None),
        P("dp", "group", "head", None),
        P("head", "dp"),
    )
    return jax.shard_map(local, mesh=mesh, in_specs=in_specs, out_specs=out_specs, check_vma=False)
```

```python
import functools
import math

import jax
import jax.numpy as jnp
from jax import lax
from jax.experimental import pallas as pl
from jax.experimental.pallas import tpu as pltpu
from jax.sharding import PartitionSpec as P

HD = 128
TXT = 128
NSTEPS = 50
SEQ = 1024
HW = 2048
D = 3072
HEADS = 8
DP = 4
GROUP = 16
TOK = SEQ // HEADS
FEAT = HW // HEADS
COLS = D // DP
CH = 256
NCH = SEQ // CH

shift_factor = 7.0
noise_level = 0.7
loss_scale = 64.0
spread_floor = 0.25
masked_score = -1e30

BF = jnp.bfloat16
F32 = jnp.float32
MESH = pl.DeviceIdType.MESH


def step_factor(step_index, rollout_count):
    current = jnp.full((8, 128), step_index.astype(F32), F32)

    def level_at(position):
        remain = 1.0 - position / NSTEPS
        return shift_factor * remain / (1.0 + (shift_factor - 1.0) * remain)

    stride = level_at(current) - level_at(current + 1.0)
    return loss_scale * jnp.sqrt(stride) / (noise_level * rollout_count)


def dot(a, b, ca, cb):
    return lax.dot_general(a, b, (((ca,), (cb,)), ((), ())), preferred_element_type=F32)


def kernel(
    q_in, k_in, v_in, n_in, p_in, rew_sm, count_sm, step_sm,
    g_out, gp_out,
    stage, qkv, nx, p_own, pring, bias_in, rbuf, fbuf, probs, kt, vt, out_t, part_s, part_own, part_r, dout_s, dout_t,
    oz, ox, wlow, yrecv, zlow, zrecv, agbuf, grads, acc_k, acc_v,
    s_in, s_qkv, r_qkv, s_nx, r_nx, s_ns, r_ns, s_p1, r_p1, s_up, r_up, s_dn, r_dn, s_pt, r_pt,
    s_rew, r_rew, s_f, r_f, s_d, r_d, s_out, r_out, s_x, r_x, s_y, r_y, s_z, r_z, s_a, r_a, s_o, r_o,
):
    x = lax.axis_index("dp")
    g = lax.axis_index("group")
    me = lax.axis_index("head")
    y = g // 2
    zlo = lax.rem(g, 2)
    zhi = me // 2
    core = lax.rem(me, 2)
    sib = me + 1 - 2 * core

    def remote(src, dst, ssem, rsem, dev):
        return pltpu.make_async_remote_copy(
            src_ref=src, dst_ref=dst, send_sem=ssem, recv_sem=rsem, device_id=dev, device_id_type=MESH
        )

    def head_peer(r):
        return (x, g, lax.rem(me + r, HEADS))

    def zhi_peer(r):
        return (x, g, lax.rem(me + 2 * r, HEADS))

    def dp_peer(r):
        return (lax.rem(x + r, DP), g, me)

    def y_peer(r):
        return (x, lax.rem(g + 2 * r, GROUP), me)

    def group_peer(r):
        return (x, lax.rem(g + r, GROUP), me)

    def z_peer(r):
        place = lax.rem(2 * zhi + zlo + r, 8)
        return (x, 2 * y + lax.rem(place, 2), 2 * (place // 2) + core)

    zlo_peer = (x, g + 1 - 2 * zlo, me)

    def rows(block, size):
        return pl.ds(pl.multiple_of(block * size, size), size)

    def each(count, make, *acts):
        def body(r, carry):
            copy = make(r)
            for act in acts:
                getattr(copy, act)()
            return carry

        lax.fori_loop(1, count, body, 0)

    barrier = pltpu.get_barrier_semaphore()

    def greet(count, peer):
        def body(r, carry):
            pl.semaphore_signal(barrier, inc=1, device_id=peer(r), device_id_type=MESH)
            return carry

        lax.fori_loop(1, count, body, 0)

    greet(HEADS, head_peer)
    greet(DP, dp_peer)
    greet(GROUP, group_peer)
    greet(4, lambda r: (x, g + 1 - 2 * zlo, lax.rem(me + 2 * r, HEADS)))

    xcols = pl.ds(pl.multiple_of(x * COLS, COLS), COLS)
    stages = [
        pltpu.make_async_copy(ref.at[0, 0], stage.at[a], s_in.at[a]) for a, ref in enumerate((q_in, k_in, v_in))
    ]
    nx_own = pltpu.make_async_copy(n_in.at[0, 0, :, xcols], nx.at[x, rows(core, TOK)], s_in.at[3])
    p_copy = pltpu.make_async_copy(p_in, p_own, s_in.at[4])
    for copy in stages:
        copy.start()
    nx_own.start()
    p_copy.start()
    rbuf[zlo, y] = jnp.full((8, 128), rew_sm[0, 0], F32)
    slot_row = lax.broadcasted_iota(jnp.int32, (TXT, CH), 0)
    bias_in[...] = jnp.where(slot_row < count_sm[0], 0.0, masked_score).astype(F32)
    pl.semaphore_wait(barrier, 7 + 3 + 15 + 3)

    def p1_copy(r):
        return remote(p_in.at[y], pring.at[y, 3 - r], s_p1.at[r], r_p1.at[r], zhi_peer(r))

    each(4, p1_copy, "start")

    def nx_copy(r):
        dst = lax.rem(x + r, DP)
        cols = pl.ds(pl.multiple_of(dst * COLS, COLS), COLS)
        return remote(
            n_in.at[0, 0, :, cols], nx.at[x, rows(core, TOK)], s_nx.at[r], r_nx.at[r], (dst, g, me)
        )

    each(DP, nx_copy, "start")
    rew_part = rbuf.at[zlo, y]
    rew_first = remote(rew_part, rew_part, s_rew.at[0], r_rew.at[0], zlo_peer)
    rew_first.start()

    pieces = ((0, 3, 0), (0, 2, 1), (2, 1, 1))

    def qkv_copy(i):
        first, count, h = pieces[i]

        def make(r):
            dst = lax.rem(me + r, HEADS)
            cols = pl.ds(pl.multiple_of(dst * FEAT + h * HD, HD), HD)
            return remote(
                stage.at[pl.ds(first, count), :, cols], qkv.at[pl.ds(first, count), h, rows(me, TOK)],
                s_qkv.at[i, r], r_qkv.at[i, r], (x, g, dst),
            )

        return make

    def qkv_own(h):
        cols = pl.ds(pl.multiple_of(me * FEAT + h * HD, HD), HD)
        return pltpu.make_async_copy(stage.at[:, :, cols], qkv.at[:, h, rows(me, TOK)], s_qkv.at[h, 0])

    def ring_up(d):
        part = pring.at[lax.rem(y + 8 - d, 8)]
        if d == 3:
            part = part.at[pl.ds(0, 2)]
        return remote(part, part, s_up.at[d], r_up.at[d], y_peer(1))

    def ring_dn(d):
        part = pring.at[lax.rem(y + d, 8)]
        if d == 3:
            part = part.at[pl.ds(2, 1)]
        return remote(part, part, s_dn.at[d], r_dn.at[d], y_peer(7))

    for copy in stages:
        copy.wait()
    each(HEADS, qkv_copy(0), "start")
    each(HEADS, qkv_copy(1), "start")
    for h in range(2):
        qkv_own(h).start()
    each(4, p1_copy, "wait_recv")
    ring_up(0).start()
    ring_dn(0).start()

    nx_own.wait()
    p_copy.wait()
    each(DP, nx_copy, "wait_recv")
    nx_part = nx.at[:, rows(core, TOK)]
    nx_sib = remote(nx_part, nx_part, s_ns.at[0], r_ns.at[0], (x, g, sib))
    nx_sib.start()
    rew_first.wait_recv()

    def rew_copy(r):
        part = rbuf.at[:, y]
        return remote(part, part, s_rew.at[r], r_rew.at[r], y_peer(r))

    each(8, rew_copy, "start")

    def part_copy(first, count, sem):
        def make(r):
            dst = lax.rem(x + r, DP)
            return remote(
                part_s.at[dst, pl.ds(first, count)], part_r.at[r, pl.ds(first, count)],
                s_pt.at[sem, r], r_pt.at[sem, r], (dst, g, me),
            )

        return make

    order = [y] + [lax.rem(y + k, 8) for k in (7, 1, 6, 2, 5, 3, 4)]
    part_groups = ((0, 1), (1, 2), (3, 2), (5, 3))

    def make_part(first, count):
        blocks = [v for b in order[first : first + count] for v in (p_own[b], pring[b].reshape(3 * 32, COLS))]
        lhs = jnp.concatenate(blocks, axis=0)

        def body(r, carry):
            k = lax.rem(x + r, DP)
            part_s[k, pl.ds(first, count)] = dot(lhs, nx[k], 1, 1).astype(BF).reshape(count, HD, CH)
            return carry

        lax.fori_loop(1, DP, body, 0)
        part_own[pl.ds(first, count)] = dot(lhs, nx[x], 1, 1).reshape(count, HD, CH)

    def sum_parts():
        for i, group in enumerate(part_groups):
            each(DP, part_copy(*group, i), "wait_recv")
            for k in range(group[0], group[0] + group[1]):
                total = part_own[k]
                for r in range(1, DP):
                    total = total + part_r[r, k].astype(F32)
                low = total.astype(BF)
                for z in range(4):
                    dout_s[z, rows(order[k], 32), :] = low[z * 32 : (z + 1) * 32]

    scale = HD ** (-0.5)

    def out_copy(h):
        def make(r):
            dst = lax.rem(zhi + r, 4)
            return remote(
                out_t.at[dst, pl.ds(h * HD, HD)], oz.at[zhi, pl.ds(h * HD, HD)],
                s_out.at[h, r], r_out.at[h, r], zhi_peer(r),
            )

        return make

    def out_own(h):
        return pltpu.make_async_copy(
            out_t.at[zhi, pl.ds(h * HD, HD)], oz.at[zhi, pl.ds(h * HD, HD)], s_out.at[h, 0]
        )

    def forward_head(h):
        qkv_own(h).wait()
        for i in ((0,), (1, 2))[h]:
            each(HEADS, qkv_copy(i), "wait_recv")
        kt[h] = qkv[1, h].T
        vt[h] = qkv[2, h].T

        def body(c, carry):
            qc = qkv[0, h, rows(c, CH), :]
            t = dot(qkv[1, h], qc, 1, 1) * (scale * math.log2(math.e))
            t = jnp.concatenate([t[: SEQ - TXT], t[SEQ - TXT :] + bias_in[...]], axis=0)
            peak = jnp.max(t, axis=0, keepdims=True)
            e = jnp.exp2(t - peak)
            total = jnp.sum(e, axis=0, keepdims=True)
            pr = e * (1.0 / total)
            probs[h, c] = pr
            part = dot(vt[h], pr.astype(BF), 1, 0)
            out_t[c, pl.ds(h * HD, HD), :] = part.astype(BF)
            return carry

        lax.fori_loop(0, NCH, body, 0)
        each(4, out_copy(h), "start")
        out_own(h).start()

    def ring_step(d):
        ring_up(d - 1).wait_recv()
        if d < 4:
            ring_up(d).start()
        ring_dn(d - 1).wait_recv()
        if d < 4:
            ring_dn(d).start()

    halves = ((0, 4), (0, 2), (2, 2))

    def x_copy(i):
        first, count = halves[i]
        feats = pl.ds(min(i, 1) * HD, HD)

        def make(r):
            return remote(
                oz.at[pl.ds(first, count), feats], ox.at[x, pl.ds(first, count), feats],
                s_x.at[i, r], r_x.at[i, r], dp_peer(r),
            )

        return make

    def x_own(h):
        feats = pl.ds(h * HD, HD)
        return pltpu.make_async_copy(oz.at[:, feats], ox.at[x, :, feats], s_x.at[h, 0])

    def share_out(h):
        out_own(h).wait()
        each(4, out_copy(h), "wait_recv")
        x_own(h).start()
        for i in ((0,), (1, 2))[h]:
            each(DP, x_copy(i), "start")

    def y_copy(i):
        first, count = halves[i]
        h = min(i, 1)

        def make(r):
            dst = lax.rem(y + r, 8)
            return remote(
                wlow.at[h, pl.ds(first, count), rows(dst, 16)], yrecv.at[h, r, pl.ds(first, count)],
                s_y.at[i, r], r_y.at[i, r], y_peer(r),
            )

        return make

    def weight(i):
        first, count = halves[i]
        h = min(i, 1)
        if i < 2:
            x_own(h).wait()
        each(DP, x_copy(i), "wait_recv")

        def body(z, carry):
            total = jnp.zeros((HD, COLS), F32)
            for k in range(DP):
                part = dot(ox[k, z, pl.ds(h * HD, HD), :], nx[k], 1, 0)
                total = total + part * fbuf[k][0:1, 0:1]
            wlow[h, z] = total.astype(BF)
            return carry

        lax.fori_loop(first, first + count, body, 0)
        each(8, y_copy(i), "start")

    def d_copy(h):
        feats = pl.ds(h * HD, HD)

        def make(r):
            return remote(
                dout_s.at[r, feats], dout_t.at[zhi, feats], s_d.at[h, r], r_d.at[h, r], zhi_peer(r)
            )

        return make

    def d_own(h):
        feats = pl.ds(h * HD, HD)
        return pltpu.make_async_copy(dout_s.at[0, feats], dout_t.at[zhi, feats], s_d.at[h, 0])

    def f_copy(r):
        return remote(fbuf.at[x], fbuf.at[x], s_f.at[r], r_f.at[r], dp_peer(r))

    def make_factor():
        each(8, rew_copy, "wait_recv")
        rewards = rbuf[...].reshape(GROUP, 8, 128)
        average = jnp.sum(rewards, axis=0) / GROUP
        variance = jnp.sum((rewards - average[None]) ** 2, axis=0) / GROUP
        base = step_factor(step_sm[0], GROUP)
        fbuf[x] = base * ((rbuf[zlo, y] - average) / jnp.maximum(jnp.sqrt(variance), spread_floor))
        each(DP, f_copy, "start")

    grad_pieces = ((0, 3, 0), (0, 1, 1), (1, 1, 1), (2, 1, 1))

    def grad_copy(i):
        first, count, h = grad_pieces[i]
        cols = pl.ds(pl.multiple_of(me * FEAT + h * HD, HD), HD)

        def make(r):
            dst = lax.rem(me + r, HEADS)
            return remote(
                grads.at[pl.ds(first, count), h, rows(dst, TOK)], g_out.at[pl.ds(first, count), :, cols],
                s_o.at[i, r], r_o.at[i, r], (x, g, dst),
            )

        return make

    def grad_own(h):
        cols = pl.ds(pl.multiple_of(me * FEAT + h * HD, HD), HD)
        return pltpu.make_async_copy(grads.at[:, h, rows(me, TOK)], g_out.at[:, :, cols], s_o.at[h, 0])

    def backward_head(h):
        factor = fbuf[x][0:1, :]
        acc_k[...] = jnp.zeros_like(acc_k)
        acc_v[...] = jnp.zeros_like(acc_v)

        def body(c, carry):
            pr = probs[h, c]
            dt = dout_t[c, pl.ds(h * HD, HD), :]
            ot = out_t[c, pl.ds(h * HD, HD), :]
            row_dot = jnp.sum(dt.astype(F32) * ot.astype(F32), axis=0, keepdims=True)
            dp = dot(qkv[2, h], dt, 1, 0)
            ds = (pr * (dp - row_dot)).astype(BF)
            gqt = dot(kt[h], ds, 1, 0)
            grads[0, h, rows(c, CH), :] = (gqt.T * (scale * factor)).astype(BF)
            acc_k[...] += dot(ds, qkv[0, h, rows(c, CH), :], 1, 0)
            acc_v[...] += dot(pr.astype(BF), dt, 1, 1)
            return carry

        lax.fori_loop(0, NCH, body, 0)
        grads[1, h] = (acc_k[...] * (scale * factor)).astype(BF)
        grads[2, h] = (acc_v[...] * factor).astype(BF)
        grad_own(h).start()

    def add_y(h):
        for i in ((0,), (1, 2))[h]:
            each(8, y_copy(i), "wait_recv")
        total = wlow[h, :, rows(y, 16), :].astype(F32)
        for r in range(1, 8):
            total = total + yrecv[h, r].astype(F32)
        for z in range(4):
            zlow[2 * z + h] = total[z].astype(BF)

    def z_copy(r):
        return remote(
            zlow.at[lax.rem(2 * zhi + zlo + r, 8)], zrecv.at[r], s_z.at[r], r_z.at[r], z_peer(r)
        )

    nx_sib.wait_recv()
    make_part(*part_groups[0])
    each(DP, part_copy(*part_groups[0], 0), "start")
    ring_step(1)
    make_part(*part_groups[1])
    each(DP, part_copy(*part_groups[1], 1), "start")
    ring_step(2)
    make_part(*part_groups[2])
    each(DP, part_copy(*part_groups[2], 2), "start")
    ring_step(3)
    forward_head(0)
    each(HEADS, qkv_copy(2), "start")
    ring_step(4)
    make_part(*part_groups[3])
    each(DP, part_copy(*part_groups[3], 3), "start")
    make_factor()
    sum_parts()
    each(4, d_copy(0), "start")
    d_own(0).start()
    share_out(0)
    forward_head(1)
    each(4, d_copy(1), "start")
    d_own(1).start()
    each(DP, f_copy, "wait_recv")
    weight(0)
    share_out(1)
    d_own(0).wait()
    each(4, d_copy(0), "wait_recv")
    backward_head(0)
    each(HEADS, grad_copy(0), "start")
    weight(1)
    weight(2)
    d_own(1).wait()
    each(4, d_copy(1), "wait_recv")
    backward_head(1)
    each(HEADS, grad_copy(1), "start")
    add_y(0)
    add_y(1)
    each(8, z_copy, "start")
    each(HEADS, grad_copy(2), "start")
    each(HEADS, grad_copy(3), "start")

    for h in range(2):
        each(4, out_copy(h), "wait_send")
        each(4, d_copy(h), "wait_send")
    for i in range(3):
        each(HEADS, qkv_copy(i), "wait_send")
        each(DP, x_copy(i), "wait_send")
        each(8, y_copy(i), "wait_send")
    for i, group in enumerate(part_groups):
        each(DP, part_copy(*group, i), "wait_send")
    for d in range(4):
        ring_up(d).wait_send()
        ring_dn(d).wait_send()
    each(4, p1_copy, "wait_send")
    each(DP, nx_copy, "wait_send")
    each(DP, f_copy, "wait_send")
    each(8, rew_copy, "wait_send")
    rew_first.wait_send()
    nx_sib.wait_send()

    each(8, z_copy, "wait_recv")
    part = zlow[2 * zhi + zlo].astype(F32)
    for r in range(1, 8):
        part = part + zrecv[r].astype(F32)
    agbuf[zlo, y] = part.astype(BF)

    def a_copy(r):
        part = agbuf.at[zlo, y]
        return remote(part, part, s_a.at[r], r_a.at[r], group_peer(r))

    each(GROUP, a_copy, "start")
    each(GROUP, a_copy, "wait_recv")
    gp_out[...] = agbuf[...].astype(F32).reshape(FEAT, COLS)

    for h in range(2):
        grad_own(h).wait()
    for i in range(4):
        each(HEADS, grad_copy(i), "wait_recv")
        each(HEADS, grad_copy(i), "wait_send")
    each(8, z_copy, "wait_send")
    each(GROUP, a_copy, "wait_send")


def local(queries, keys, values, noise, projection, rewards, counts, step_index):
    hbm = pl.BlockSpec(memory_space=pl.ANY)
    vmem = pl.BlockSpec(memory_space=pltpu.VMEM)
    smem = pl.BlockSpec(memory_space=pltpu.SMEM)
    dma = pltpu.SemaphoreType.DMA
    grads, grad_projection = pl.pallas_call(
        kernel,
        out_shape=(jax.ShapeDtypeStruct((3, TOK, HW), BF), jax.ShapeDtypeStruct((FEAT, COLS), F32)),
        in_specs=[hbm] * 5 + [smem] * 3,
        out_specs=(hbm, vmem),
        scratch_shapes=[
            pltpu.VMEM((3, TOK, HW), BF),
            pltpu.VMEM((3, 2, SEQ, HD), BF),
            pltpu.VMEM((DP, 2 * TOK, COLS), BF),
            pltpu.VMEM((8, 32, COLS), BF),
            pltpu.VMEM((8, 3, 32, COLS), BF),
            pltpu.VMEM((TXT, CH), F32),
            pltpu.VMEM((2, 8, 8, 128), F32),
            pltpu.VMEM((DP, 8, 128), F32),
            pltpu.VMEM((2, NCH, SEQ, CH), F32),
            pltpu.VMEM((2, HD, SEQ), BF),
            pltpu.VMEM((2, HD, SEQ), BF),
            pltpu.VMEM((NCH, FEAT, CH), BF),
            pltpu.VMEM((DP, 8, HD, CH), BF),
            pltpu.VMEM((8, HD, CH), F32),
            pltpu.VMEM((DP, 8, HD, CH), BF),
            pltpu.VMEM((NCH, FEAT, CH), BF),
            pltpu.VMEM((NCH, FEAT, CH), BF),
            pltpu.VMEM((NCH, FEAT, CH), BF),
            pltpu.VMEM((DP, NCH, FEAT, CH), BF),
            pltpu.VMEM((2, 4, HD, COLS), BF),
            pltpu.VMEM((2, 8, 4, 16, COLS), BF),
            pltpu.VMEM((8, 16, COLS), BF),
            pltpu.VMEM((8, 16, COLS), BF),
            pltpu.VMEM((2, 8, 16, COLS), BF),
            pltpu.VMEM((3, 2, SEQ, HD), BF),
            pltpu.VMEM((SEQ, HD), F32),
            pltpu.VMEM((SEQ, HD), F32),
            dma((5,)),
            dma((3, HEADS)), dma((3, HEADS)),
            dma((DP,)), dma((DP,)),
            dma((1,)), dma((1,)),
            dma((4,)), dma((4,)),
            dma((4,)), dma((4,)),
            dma((4,)), dma((4,)),
            dma((4, DP)), dma((4, DP)),
            dma((8,)), dma((8,)),
            dma((DP,)), dma((DP,)),
            dma((2, 4)), dma((2, 4)),
            dma((2, 4)), dma((2, 4)),
            dma((3, DP)), dma((3, DP)),
            dma((3, 8)), dma((3, 8)),
            dma((8,)), dma((8,)),
            dma((GROUP,)), dma((GROUP,)),
            dma((4, HEADS)), dma((4, HEADS)),
        ],
        compiler_params=pltpu.CompilerParams(
            collective_id=0, has_side_effects=True, vmem_limit_bytes=58 << 20
        ),
        name="rollout_grads",
    )(queries, keys, values, noise, projection.reshape(8, 32, COLS), rewards, counts, step_index)
    return (*(grads[a][None, None] for a in range(3)), grad_projection)


def solution(mesh):
    in_specs = (
        P("dp", "group", "head", None),
        P("dp", "group", "head", None),
        P("dp", "group", "head", None),
        P("dp", "group", "head", None),
        P("head", "dp"),
        P("dp", "group"),
        P("dp"),
        P(),
    )
    out_specs = (
        P("dp", "group", "head", None),
        P("dp", "group", "head", None),
        P("dp", "group", "head", None),
        P("head", "dp"),
    )
    return jax.shard_map(local, mesh=mesh, in_specs=in_specs, out_specs=out_specs, check_vma=False)
```

```python
import functools
import math

import jax
import jax.numpy as jnp
from jax import lax
from jax.experimental import pallas as pl
from jax.experimental.pallas import tpu as pltpu
from jax.sharding import PartitionSpec as P

HD = 128
TXT = 128
NSTEPS = 50
SEQ = 1024
HW = 2048
D = 3072
HEADS = 8
DP = 4
GROUP = 16
TOK = SEQ // HEADS
FEAT = HW // HEADS
COLS = D // DP
CH = 256
NCH = SEQ // CH

shift_factor = 7.0
noise_level = 0.7
loss_scale = 64.0
spread_floor = 0.25
masked_score = -1e30

BF = jnp.bfloat16
F32 = jnp.float32
MESH = pl.DeviceIdType.MESH


def step_factor(step_index, rollout_count):
    current = jnp.full((8, 128), step_index.astype(F32), F32)

    def level_at(position):
        remain = 1.0 - position / NSTEPS
        return shift_factor * remain / (1.0 + (shift_factor - 1.0) * remain)

    stride = level_at(current) - level_at(current + 1.0)
    return loss_scale * jnp.sqrt(stride) / (noise_level * rollout_count)


def dot(a, b, ca, cb):
    return lax.dot_general(a, b, (((ca,), (cb,)), ((), ())), preferred_element_type=F32)


def kernel(
    q_in, k_in, v_in, n_in, p_in, rew_sm, count_sm, step_sm,
    g_out, gp_out,
    stage, qkv, nx, p_own, pring, bias_in, rbuf, fbuf, probs, kt, vt, out_t, part_s, part_own, part_r, dout_s, dout_t,
    oz, ox, wlow, yrecv, zlow, zrecv, agbuf, grads, acc_k, acc_v,
    s_in, s_qkv, r_qkv, s_nx, r_nx, s_ns, r_ns, s_p1, r_p1, s_up, r_up, s_dn, r_dn, s_pt, r_pt,
    s_rew, r_rew, s_f, r_f, s_d, r_d, s_out, r_out, s_x, r_x, s_y, r_y, s_z, r_z, s_a, r_a, s_o, r_o,
):
    x = lax.axis_index("dp")
    g = lax.axis_index("group")
    me = lax.axis_index("head")
    y = g // 2
    zlo = lax.rem(g, 2)
    zhi = me // 2
    core = lax.rem(me, 2)
    sib = me + 1 - 2 * core

    def remote(src, dst, ssem, rsem, dev):
        return pltpu.make_async_remote_copy(
            src_ref=src, dst_ref=dst, send_sem=ssem, recv_sem=rsem, device_id=dev, device_id_type=MESH
        )

    def head_peer(r):
        return (x, g, lax.rem(me + r, HEADS))

    def zhi_peer(r):
        return (x, g, lax.rem(me + 2 * r, HEADS))

    def dp_peer(r):
        return (lax.rem(x + r, DP), g, me)

    def y_peer(r):
        return (x, lax.rem(g + 2 * r, GROUP), me)

    def group_peer(r):
        return (x, lax.rem(g + r, GROUP), me)

    def z_peer(r):
        place = lax.rem(2 * zhi + zlo + r, 8)
        return (x, 2 * y + lax.rem(place, 2), 2 * (place // 2) + core)

    zlo_peer = (x, g + 1 - 2 * zlo, me)

    def rows(block, size):
        return pl.ds(pl.multiple_of(block * size, size), size)

    def each(count, make, *acts):
        def body(r, carry):
            copy = make(r)
            for act in acts:
                getattr(copy, act)()
            return carry

        lax.fori_loop(1, count, body, 0)

    barrier = pltpu.get_barrier_semaphore()

    def greet(count, peer):
        def body(r, carry):
            pl.semaphore_signal(barrier, inc=1, device_id=peer(r), device_id_type=MESH)
            return carry

        lax.fori_loop(1, count, body, 0)

    greet(HEADS, head_peer)
    greet(DP, dp_peer)
    greet(GROUP, group_peer)
    greet(4, lambda r: (x, g + 1 - 2 * zlo, lax.rem(me + 2 * r, HEADS)))

    xcols = pl.ds(pl.multiple_of(x * COLS, COLS), COLS)
    stages = [
        pltpu.make_async_copy(ref.at[0, 0], stage.at[a], s_in.at[a]) for a, ref in enumerate((q_in, k_in, v_in))
    ]
    nx_own = pltpu.make_async_copy(n_in.at[0, 0, :, xcols], nx.at[x, rows(core, TOK)], s_in.at[3])
    p_copy = pltpu.make_async_copy(p_in, p_own, s_in.at[4])
    for copy in stages:
        copy.start()
    nx_own.start()
    p_copy.start()
    rbuf[zlo, y] = jnp.full((8, 128), rew_sm[0, 0], F32)
    slot_row = lax.broadcasted_iota(jnp.int32, (TXT, CH), 0)
    bias_in[...] = jnp.where(slot_row < count_sm[0], 0.0, masked_score).astype(F32)
    pl.semaphore_wait(barrier, 7 + 3 + 15 + 3)

    def p1_copy(r):
        return remote(p_in.at[y], pring.at[y, 3 - r], s_p1.at[r], r_p1.at[r], zhi_peer(r))

    each(4, p1_copy, "start")

    def nx_copy(r):
        dst = lax.rem(x + r, DP)
        cols = pl.ds(pl.multiple_of(dst * COLS, COLS), COLS)
        return remote(
            n_in.at[0, 0, :, cols], nx.at[x, rows(core, TOK)], s_nx.at[r], r_nx.at[r], (dst, g, me)
        )

    each(DP, nx_copy, "start")
    rew_part = rbuf.at[zlo, y]
    rew_first = remote(rew_part, rew_part, s_rew.at[0], r_rew.at[0], zlo_peer)
    rew_first.start()

    pieces = ((0, 3, 0), (0, 1, 1), (1, 2, 1))

    def qkv_copy(i):
        first, count, h = pieces[i]

        def make(r):
            dst = lax.rem(me + r, HEADS)
            cols = pl.ds(pl.multiple_of(dst * FEAT + h * HD, HD), HD)
            return remote(
                stage.at[pl.ds(first, count), :, cols], qkv.at[pl.ds(first, count), h, rows(me, TOK)],
                s_qkv.at[i, r], r_qkv.at[i, r], (x, g, dst),
            )

        return make

    def qkv_own(h):
        cols = pl.ds(pl.multiple_of(me * FEAT + h * HD, HD), HD)
        return pltpu.make_async_copy(stage.at[:, :, cols], qkv.at[:, h, rows(me, TOK)], s_qkv.at[h, 0])

    def ring_up(d):
        part = pring.at[lax.rem(y + 8 - d, 8)]
        if d == 3:
            part = part.at[pl.ds(0, 2)]
        return remote(part, part, s_up.at[d], r_up.at[d], y_peer(1))

    def ring_dn(d):
        part = pring.at[lax.rem(y + d, 8)]
        if d == 3:
            part = part.at[pl.ds(2, 1)]
        return remote(part, part, s_dn.at[d], r_dn.at[d], y_peer(7))

    for copy in stages:
        copy.wait()
    each(HEADS, qkv_copy(0), "start")
    each(HEADS, qkv_copy(1), "start")
    for h in range(2):
        qkv_own(h).start()
    each(4, p1_copy, "wait_recv")
    ring_up(0).start()
    ring_dn(0).start()

    nx_own.wait()
    p_copy.wait()
    each(DP, nx_copy, "wait_recv")
    nx_part = nx.at[:, rows(core, TOK)]
    nx_sib = remote(nx_part, nx_part, s_ns.at[0], r_ns.at[0], (x, g, sib))
    nx_sib.start()
    rew_first.wait_recv()

    def rew_copy(r):
        part = rbuf.at[:, y]
        return remote(part, part, s_rew.at[r], r_rew.at[r], y_peer(r))

    each(8, rew_copy, "start")

    def part_copy(first, count, sem):
        def make(r):
            dst = lax.rem(x + r, DP)
            return remote(
                part_s.at[dst, pl.ds(first, count)], part_r.at[r, pl.ds(first, count)],
                s_pt.at[sem, r], r_pt.at[sem, r], (dst, g, me),
            )

        return make

    order = [y] + [lax.rem(y + k, 8) for k in (7, 1, 6, 2, 5, 3, 4)]
    part_groups = ((0, 1), (1, 2), (3, 2), (5, 3))

    def make_part(first, count):
        blocks = [v for b in order[first : first + count] for v in (p_own[b], pring[b].reshape(3 * 32, COLS))]
        lhs = jnp.concatenate(blocks, axis=0)

        def body(r, carry):
            k = lax.rem(x + r, DP)
            part_s[k, pl.ds(first, count)] = dot(lhs, nx[k], 1, 1).astype(BF).reshape(count, HD, CH)
            return carry

        lax.fori_loop(1, DP, body, 0)
        part_own[pl.ds(first, count)] = dot(lhs, nx[x], 1, 1).reshape(count, HD, CH)

    def sum_parts():
        for i, group in enumerate(part_groups):
            each(DP, part_copy(*group, i), "wait_recv")
            for k in range(group[0], group[0] + group[1]):
                total = part_own[k]
                for r in range(1, DP):
                    total = total + part_r[r, k].astype(F32)
                low = total.astype(BF)
                for z in range(4):
                    dout_s[z, rows(order[k], 32), :] = low[z * 32 : (z + 1) * 32]

    scale = HD ** (-0.5)

    def out_copy(h):
        def make(r):
            dst = lax.rem(zhi + r, 4)
            return remote(
                out_t.at[dst, pl.ds(h * HD, HD)], oz.at[zhi, pl.ds(h * HD, HD)],
                s_out.at[h, r], r_out.at[h, r], zhi_peer(r),
            )

        return make

    def out_own(h):
        return pltpu.make_async_copy(
            out_t.at[zhi, pl.ds(h * HD, HD)], oz.at[zhi, pl.ds(h * HD, HD)], s_out.at[h, 0]
        )

    def forward_head(h):
        qkv_own(h).wait()
        for i in ((0,), (1, 2))[h]:
            each(HEADS, qkv_copy(i), "wait_recv")
        kt[h] = qkv[1, h].T
        vt[h] = qkv[2, h].T

        def body(c, carry):
            qc = qkv[0, h, rows(c, CH), :]
            t = dot(qkv[1, h], qc, 1, 1) * (scale * math.log2(math.e))
            t = jnp.concatenate([t[: SEQ - TXT], t[SEQ - TXT :] + bias_in[...]], axis=0)
            peak = jnp.max(t, axis=0, keepdims=True)
            e = jnp.exp2(t - peak)
            total = jnp.sum(e, axis=0, keepdims=True)
            pr = e * (1.0 / total)
            probs[h, c] = pr
            part = dot(vt[h], pr.astype(BF), 1, 0)
            out_t[c, pl.ds(h * HD, HD), :] = part.astype(BF)
            return carry

        lax.fori_loop(0, NCH, body, 0)
        each(4, out_copy(h), "start")
        out_own(h).start()

    def ring_step(d):
        ring_up(d - 1).wait_recv()
        if d < 4:
            ring_up(d).start()
        ring_dn(d - 1).wait_recv()
        if d < 4:
            ring_dn(d).start()

    halves = ((0, 4), (0, 2), (2, 2))

    def x_copy(i):
        first, count = halves[i]
        feats = pl.ds(min(i, 1) * HD, HD)

        def make(r):
            return remote(
                oz.at[pl.ds(first, count), feats], ox.at[x, pl.ds(first, count), feats],
                s_x.at[i, r], r_x.at[i, r], dp_peer(r),
            )

        return make

    def x_own(h):
        feats = pl.ds(h * HD, HD)
        return pltpu.make_async_copy(oz.at[:, feats], ox.at[x, :, feats], s_x.at[h, 0])

    def share_out(h):
        out_own(h).wait()
        each(4, out_copy(h), "wait_recv")
        x_own(h).start()
        for i in ((0,), (1, 2))[h]:
            each(DP, x_copy(i), "start")

    def y_copy(i):
        first, count = halves[i]
        h = min(i, 1)

        def make(r):
            dst = lax.rem(y + r, 8)
            return remote(
                wlow.at[h, pl.ds(first, count), rows(dst, 16)], yrecv.at[h, r, pl.ds(first, count)],
                s_y.at[i, r], r_y.at[i, r], y_peer(r),
            )

        return make

    def weight(i):
        first, count = halves[i]
        h = min(i, 1)
        if i < 2:
            x_own(h).wait()
        each(DP, x_copy(i), "wait_recv")

        def body(z, carry):
            total = jnp.zeros((HD, COLS), F32)
            for k in range(DP):
                part = dot(ox[k, z, pl.ds(h * HD, HD), :], nx[k], 1, 0)
                total = total + part * fbuf[k][0:1, 0:1]
            wlow[h, z] = total.astype(BF)
            return carry

        lax.fori_loop(first, first + count, body, 0)
        each(8, y_copy(i), "start")

    def d_copy(h):
        feats = pl.ds(h * HD, HD)

        def make(r):
            return remote(
                dout_s.at[r, feats], dout_t.at[zhi, feats], s_d.at[h, r], r_d.at[h, r], zhi_peer(r)
            )

        return make

    def d_own(h):
        feats = pl.ds(h * HD, HD)
        return pltpu.make_async_copy(dout_s.at[0, feats], dout_t.at[zhi, feats], s_d.at[h, 0])

    def f_copy(r):
        return remote(fbuf.at[x], fbuf.at[x], s_f.at[r], r_f.at[r], dp_peer(r))

    def make_factor():
        each(8, rew_copy, "wait_recv")
        rewards = rbuf[...].reshape(GROUP, 8, 128)
        average = jnp.sum(rewards, axis=0) / GROUP
        variance = jnp.sum((rewards - average[None]) ** 2, axis=0) / GROUP
        base = step_factor(step_sm[0], GROUP)
        fbuf[x] = base * ((rbuf[zlo, y] - average) / jnp.maximum(jnp.sqrt(variance), spread_floor))
        each(DP, f_copy, "start")

    grad_pieces = ((0, 3, 0), (0, 1, 1), (1, 1, 1), (2, 1, 1))

    def grad_copy(i):
        first, count, h = grad_pieces[i]
        cols = pl.ds(pl.multiple_of(me * FEAT + h * HD, HD), HD)

        def make(r):
            dst = lax.rem(me + r, HEADS)
            return remote(
                grads.at[pl.ds(first, count), h, rows(dst, TOK)], g_out.at[pl.ds(first, count), :, cols],
                s_o.at[i, r], r_o.at[i, r], (x, g, dst),
            )

        return make

    def grad_own(h):
        cols = pl.ds(pl.multiple_of(me * FEAT + h * HD, HD), HD)
        return pltpu.make_async_copy(grads.at[:, h, rows(me, TOK)], g_out.at[:, :, cols], s_o.at[h, 0])

    def backward_head(h):
        factor = fbuf[x][0:1, :]
        acc_k[...] = jnp.zeros_like(acc_k)
        acc_v[...] = jnp.zeros_like(acc_v)

        def body(c, carry):
            pr = probs[h, c]
            dt = dout_t[c, pl.ds(h * HD, HD), :]
            ot = out_t[c, pl.ds(h * HD, HD), :]
            row_dot = jnp.sum(dt.astype(F32) * ot.astype(F32), axis=0, keepdims=True)
            dp = dot(qkv[2, h], dt, 1, 0)
            ds = (pr * (dp - row_dot)).astype(BF)
            gqt = dot(kt[h], ds, 1, 0)
            grads[0, h, rows(c, CH), :] = (gqt.T * (scale * factor)).astype(BF)
            acc_k[...] += dot(ds, qkv[0, h, rows(c, CH), :], 1, 0)
            acc_v[...] += dot(pr.astype(BF), dt, 1, 1)
            return carry

        lax.fori_loop(0, NCH, body, 0)
        grads[1, h] = (acc_k[...] * (scale * factor)).astype(BF)
        grads[2, h] = (acc_v[...] * factor).astype(BF)
        grad_own(h).start()

    def add_y(h):
        for i in ((0,), (1, 2))[h]:
            each(8, y_copy(i), "wait_recv")
        total = wlow[h, :, rows(y, 16), :].astype(F32)
        for r in range(1, 8):
            total = total + yrecv[h, r].astype(F32)
        for z in range(4):
            zlow[2 * z + h] = total[z].astype(BF)

    def z_copy(r):
        return remote(
            zlow.at[lax.rem(2 * zhi + zlo + r, 8)], zrecv.at[r], s_z.at[r], r_z.at[r], z_peer(r)
        )

    def send_z(h):
        @pl.when(zlo == h)
        def near():
            for r in (2, 4, 6):
                z_copy(r).start()

        @pl.when(zlo != h)
        def far():
            for r in (1, 3, 5, 7):
                z_copy(r).start()

    def a_copy(r):
        part = agbuf.at[zlo, y]
        return remote(part, part, s_a.at[r], r_a.at[r], group_peer(r))

    def add_z(h):
        @pl.when(zlo == h)
        def last():
            each(8, z_copy, "wait_recv")
            part = zlow[2 * zhi + zlo].astype(F32)
            for r in range(1, 8):
                part = part + zrecv[r].astype(F32)
            agbuf[zlo, y] = part.astype(BF)
            each(GROUP, a_copy, "start")

    nx_sib.wait_recv()
    make_part(*part_groups[0])
    each(DP, part_copy(*part_groups[0], 0), "start")
    ring_step(1)
    make_part(*part_groups[1])
    each(DP, part_copy(*part_groups[1], 1), "start")
    ring_step(2)
    make_part(*part_groups[2])
    each(DP, part_copy(*part_groups[2], 2), "start")
    ring_step(3)
    forward_head(0)
    each(HEADS, qkv_copy(2), "start")
    ring_step(4)
    make_part(*part_groups[3])
    each(DP, part_copy(*part_groups[3], 3), "start")
    make_factor()
    share_out(0)
    sum_parts()
    forward_head(1)
    each(4, d_copy(0), "start")
    d_own(0).start()
    each(4, d_copy(1), "start")
    d_own(1).start()
    each(DP, f_copy, "wait_recv")
    weight(0)
    share_out(1)
    d_own(0).wait()
    each(4, d_copy(0), "wait_recv")
    backward_head(0)
    each(HEADS, grad_copy(0), "start")
    weight(1)
    weight(2)
    add_y(0)
    send_z(0)
    d_own(1).wait()
    each(4, d_copy(1), "wait_recv")
    backward_head(1)
    each(HEADS, grad_copy(1), "start")
    add_z(0)
    add_y(1)
    send_z(1)
    each(HEADS, grad_copy(2), "start")
    add_z(1)
    each(HEADS, grad_copy(3), "start")

    for h in range(2):
        each(4, out_copy(h), "wait_send")
        each(4, d_copy(h), "wait_send")
    for i in range(3):
        each(HEADS, qkv_copy(i), "wait_send")
        each(DP, x_copy(i), "wait_send")
        each(8, y_copy(i), "wait_send")
    for i, group in enumerate(part_groups):
        each(DP, part_copy(*group, i), "wait_send")
    for d in range(4):
        ring_up(d).wait_send()
        ring_dn(d).wait_send()
    each(4, p1_copy, "wait_send")
    each(DP, nx_copy, "wait_send")
    each(DP, f_copy, "wait_send")
    each(8, rew_copy, "wait_send")
    rew_first.wait_send()
    nx_sib.wait_send()

    each(GROUP, a_copy, "wait_recv")
    gp_out[...] = agbuf[...].astype(F32).reshape(FEAT, COLS)

    for h in range(2):
        grad_own(h).wait()
    for i in range(4):
        each(HEADS, grad_copy(i), "wait_recv")
        each(HEADS, grad_copy(i), "wait_send")
    each(8, z_copy, "wait_send")
    each(GROUP, a_copy, "wait_send")


def local(queries, keys, values, noise, projection, rewards, counts, step_index):
    hbm = pl.BlockSpec(memory_space=pl.ANY)
    vmem = pl.BlockSpec(memory_space=pltpu.VMEM)
    smem = pl.BlockSpec(memory_space=pltpu.SMEM)
    dma = pltpu.SemaphoreType.DMA
    grads, grad_projection = pl.pallas_call(
        kernel,
        out_shape=(jax.ShapeDtypeStruct((3, TOK, HW), BF), jax.ShapeDtypeStruct((FEAT, COLS), F32)),
        in_specs=[hbm] * 5 + [smem] * 3,
        out_specs=(hbm, vmem),
        scratch_shapes=[
            pltpu.VMEM((3, TOK, HW), BF),
            pltpu.VMEM((3, 2, SEQ, HD), BF),
            pltpu.VMEM((DP, 2 * TOK, COLS), BF),
            pltpu.VMEM((8, 32, COLS), BF),
            pltpu.VMEM((8, 3, 32, COLS), BF),
            pltpu.VMEM((TXT, CH), F32),
            pltpu.VMEM((2, 8, 8, 128), F32),
            pltpu.VMEM((DP, 8, 128), F32),
            pltpu.VMEM((2, NCH, SEQ, CH), F32),
            pltpu.VMEM((2, HD, SEQ), BF),
            pltpu.VMEM((2, HD, SEQ), BF),
            pltpu.VMEM((NCH, FEAT, CH), BF),
            pltpu.VMEM((DP, 8, HD, CH), BF),
            pltpu.VMEM((8, HD, CH), F32),
            pltpu.VMEM((DP, 8, HD, CH), BF),
            pltpu.VMEM((NCH, FEAT, CH), BF),
            pltpu.VMEM((NCH, FEAT, CH), BF),
            pltpu.VMEM((NCH, FEAT, CH), BF),
            pltpu.VMEM((DP, NCH, FEAT, CH), BF),
            pltpu.VMEM((2, 4, HD, COLS), BF),
            pltpu.VMEM((2, 8, 4, 16, COLS), BF),
            pltpu.VMEM((8, 16, COLS), BF),
            pltpu.VMEM((8, 16, COLS), BF),
            pltpu.VMEM((2, 8, 16, COLS), BF),
            pltpu.VMEM((3, 2, SEQ, HD), BF),
            pltpu.VMEM((SEQ, HD), F32),
            pltpu.VMEM((SEQ, HD), F32),
            dma((5,)),
            dma((3, HEADS)), dma((3, HEADS)),
            dma((DP,)), dma((DP,)),
            dma((1,)), dma((1,)),
            dma((4,)), dma((4,)),
            dma((4,)), dma((4,)),
            dma((4,)), dma((4,)),
            dma((4, DP)), dma((4, DP)),
            dma((8,)), dma((8,)),
            dma((DP,)), dma((DP,)),
            dma((2, 4)), dma((2, 4)),
            dma((2, 4)), dma((2, 4)),
            dma((3, DP)), dma((3, DP)),
            dma((3, 8)), dma((3, 8)),
            dma((8,)), dma((8,)),
            dma((GROUP,)), dma((GROUP,)),
            dma((4, HEADS)), dma((4, HEADS)),
        ],
        compiler_params=pltpu.CompilerParams(
            collective_id=0, has_side_effects=True, vmem_limit_bytes=58 << 20
        ),
        name="rollout_grads",
    )(queries, keys, values, noise, projection.reshape(8, 32, COLS), rewards, counts, step_index)
    return (*(grads[a][None, None] for a in range(3)), grad_projection)


def solution(mesh):
    in_specs = (
        P("dp", "group", "head", None),
        P("dp", "group", "head", None),
        P("dp", "group", "head", None),
        P("dp", "group", "head", None),
        P("head", "dp"),
        P("dp", "group"),
        P("dp"),
        P(),
    )
    out_specs = (
        P("dp", "group", "head", None),
        P("dp", "group", "head", None),
        P("dp", "group", "head", None),
        P("head", "dp"),
    )
    return jax.shard_map(local, mesh=mesh, in_specs=in_specs, out_specs=out_specs, check_vma=False)
```

```python
import functools
import math

import jax
import jax.numpy as jnp
from jax import lax
from jax.experimental import pallas as pl
from jax.experimental.pallas import tpu as pltpu
from jax.sharding import PartitionSpec as P

HD = 128
TXT = 128
NSTEPS = 50
SEQ = 1024
HW = 2048
D = 3072
HEADS = 8
DP = 4
GROUP = 16
TOK = SEQ // HEADS
FEAT = HW // HEADS
COLS = D // DP
CH = 256
NCH = SEQ // CH

shift_factor = 7.0
noise_level = 0.7
loss_scale = 64.0
spread_floor = 0.25
masked_score = -1e30

BF = jnp.bfloat16
F32 = jnp.float32
MESH = pl.DeviceIdType.MESH


def step_factor(step_index, rollout_count):
    current = jnp.full((8, 128), step_index.astype(F32), F32)

    def level_at(position):
        remain = 1.0 - position / NSTEPS
        return shift_factor * remain / (1.0 + (shift_factor - 1.0) * remain)

    stride = level_at(current) - level_at(current + 1.0)
    return loss_scale * jnp.sqrt(stride) / (noise_level * rollout_count)


def dot(a, b, ca, cb):
    return lax.dot_general(a, b, (((ca,), (cb,)), ((), ())), preferred_element_type=F32)


def kernel(
    q_in, k_in, v_in, n_in, p_in, rew_sm, count_sm, step_sm,
    g_out, gp_out,
    stage, qkv, nx, p_own, pring, bias_in, rbuf, fbuf, probs, kt, vt, out_t, part_s, part_own, part_r, dout_s, dout_t,
    oz, ox, wlow, yrecv, zlow, zrecv, agbuf, grads, acc_k, acc_v,
    s_in, s_qkv, r_qkv, s_nx, r_nx, s_ns, r_ns, s_p1, r_p1, s_up, r_up, s_dn, r_dn, s_pt, r_pt,
    s_rew, r_rew, s_f, r_f, s_d, r_d, s_out, r_out, s_x, r_x, s_y, r_y, s_z, r_z, s_a, r_a, s_o, r_o,
):
    x = lax.axis_index("dp")
    g = lax.axis_index("group")
    me = lax.axis_index("head")
    y = g // 2
    zlo = lax.rem(g, 2)
    zhi = me // 2
    core = lax.rem(me, 2)
    sib = me + 1 - 2 * core

    def remote(src, dst, ssem, rsem, dev):
        return pltpu.make_async_remote_copy(
            src_ref=src, dst_ref=dst, send_sem=ssem, recv_sem=rsem, device_id=dev, device_id_type=MESH
        )

    def head_peer(r):
        return (x, g, lax.rem(me + r, HEADS))

    def zhi_peer(r):
        return (x, g, lax.rem(me + 2 * r, HEADS))

    def dp_peer(r):
        return (lax.rem(x + r, DP), g, me)

    def y_peer(r):
        return (x, lax.rem(g + 2 * r, GROUP), me)

    def group_peer(r):
        return (x, lax.rem(g + r, GROUP), me)

    def z_peer(r):
        place = lax.rem(2 * zhi + zlo + r, 8)
        return (x, 2 * y + lax.rem(place, 2), 2 * (place // 2) + core)

    zlo_peer = (x, g + 1 - 2 * zlo, me)

    def rows(block, size):
        return pl.ds(pl.multiple_of(block * size, size), size)

    def each(count, make, *acts):
        def body(r, carry):
            copy = make(r)
            for act in acts:
                getattr(copy, act)()
            return carry

        lax.fori_loop(1, count, body, 0)

    barrier = pltpu.get_barrier_semaphore()

    def greet(count, peer):
        def body(r, carry):
            pl.semaphore_signal(barrier, inc=1, device_id=peer(r), device_id_type=MESH)
            return carry

        lax.fori_loop(1, count, body, 0)

    greet(HEADS, head_peer)
    greet(DP, dp_peer)
    greet(GROUP, group_peer)
    greet(4, lambda r: (x, g + 1 - 2 * zlo, lax.rem(me + 2 * r, HEADS)))

    xcols = pl.ds(pl.multiple_of(x * COLS, COLS), COLS)
    stages = [
        pltpu.make_async_copy(ref.at[0, 0], stage.at[a], s_in.at[a]) for a, ref in enumerate((q_in, k_in, v_in))
    ]
    nx_own = pltpu.make_async_copy(n_in.at[0, 0, :, xcols], nx.at[x, rows(core, TOK)], s_in.at[3])
    p_copy = pltpu.make_async_copy(p_in, p_own, s_in.at[4])
    for copy in stages:
        copy.start()
    nx_own.start()
    p_copy.start()
    rbuf[zlo, y] = jnp.full((8, 128), rew_sm[0, 0], F32)
    slot_row = lax.broadcasted_iota(jnp.int32, (TXT, CH), 0)
    bias_in[...] = jnp.where(slot_row < count_sm[0], 0.0, masked_score).astype(F32)
    pl.semaphore_wait(barrier, 7 + 3 + 15 + 3)

    def p1_copy(r):
        return remote(p_in.at[y], pring.at[y, 3 - r], s_p1.at[r], r_p1.at[r], zhi_peer(r))

    each(4, p1_copy, "start")

    def nx_copy(r):
        dst = lax.rem(x + r, DP)
        cols = pl.ds(pl.multiple_of(dst * COLS, COLS), COLS)
        return remote(
            n_in.at[0, 0, :, cols], nx.at[x, rows(core, TOK)], s_nx.at[r], r_nx.at[r], (dst, g, me)
        )

    each(DP, nx_copy, "start")
    rew_part = rbuf.at[zlo, y]
    rew_first = remote(rew_part, rew_part, s_rew.at[0], r_rew.at[0], zlo_peer)
    rew_first.start()

    pieces = ((0, 3, 0), (0, 1, 1), (1, 2, 1))

    def qkv_copy(i):
        first, count, h = pieces[i]

        def make(r):
            dst = lax.rem(me + r, HEADS)
            cols = pl.ds(pl.multiple_of(dst * FEAT + h * HD, HD), HD)
            return remote(
                stage.at[pl.ds(first, count), :, cols], qkv.at[pl.ds(first, count), h, rows(me, TOK)],
                s_qkv.at[i, r], r_qkv.at[i, r], (x, g, dst),
            )

        return make

    def qkv_own(h):
        cols = pl.ds(pl.multiple_of(me * FEAT + h * HD, HD), HD)
        return pltpu.make_async_copy(stage.at[:, :, cols], qkv.at[:, h, rows(me, TOK)], s_qkv.at[h, 0])

    def ring_up(d):
        part = pring.at[lax.rem(y + 8 - d, 8)]
        if d == 3:
            part = part.at[pl.ds(0, 2)]
        return remote(part, part, s_up.at[d], r_up.at[d], y_peer(1))

    def ring_dn(d):
        part = pring.at[lax.rem(y + d, 8)]
        if d == 3:
            part = part.at[pl.ds(2, 1)]
        return remote(part, part, s_dn.at[d], r_dn.at[d], y_peer(7))

    for copy in stages:
        copy.wait()
    each(HEADS, qkv_copy(0), "start")
    each(HEADS, qkv_copy(1), "start")
    for h in range(2):
        qkv_own(h).start()
    each(4, p1_copy, "wait_recv")
    ring_up(0).start()
    ring_dn(0).start()

    nx_own.wait()
    p_copy.wait()
    each(DP, nx_copy, "wait_recv")
    nx_part = nx.at[:, rows(core, TOK)]
    nx_sib = remote(nx_part, nx_part, s_ns.at[0], r_ns.at[0], (x, g, sib))
    nx_sib.start()
    rew_first.wait_recv()

    def rew_copy(r):
        part = rbuf.at[:, y]
        return remote(part, part, s_rew.at[r], r_rew.at[r], y_peer(r))

    each(8, rew_copy, "start")

    def part_copy(first, count, sem):
        def make(r):
            dst = lax.rem(x + r, DP)
            return remote(
                part_s.at[dst, pl.ds(first, count)], part_r.at[r, pl.ds(first, count)],
                s_pt.at[sem, r], r_pt.at[sem, r], (dst, g, me),
            )

        return make

    order = [y] + [lax.rem(y + k, 8) for k in (7, 1, 6, 2, 5, 3, 4)]
    part_groups = ((0, 1), (1, 2), (3, 2), (5, 3))

    def make_part(first, count):
        blocks = [v for b in order[first : first + count] for v in (p_own[b], pring[b].reshape(3 * 32, COLS))]
        lhs = jnp.concatenate(blocks, axis=0)

        def body(r, carry):
            k = lax.rem(x + r, DP)
            part_s[k, pl.ds(first, count)] = dot(lhs, nx[k], 1, 1).astype(BF).reshape(count, HD, CH)
            return carry

        lax.fori_loop(1, DP, body, 0)
        part_own[pl.ds(first, count)] = dot(lhs, nx[x], 1, 1).reshape(count, HD, CH)

    def sum_parts():
        for i, group in enumerate(part_groups):
            each(DP, part_copy(*group, i), "wait_recv")
            for k in range(group[0], group[0] + group[1]):
                total = part_own[k]
                for r in range(1, DP):
                    total = total + part_r[r, k].astype(F32)
                low = total.astype(BF)
                for z in range(4):
                    dout_s[z, rows(order[k], 32), :] = low[z * 32 : (z + 1) * 32]

    scale = HD ** (-0.5)

    def out_copy(h):
        def make(r):
            dst = lax.rem(zhi + r, 4)
            return remote(
                out_t.at[dst, pl.ds(h * HD, HD)], oz.at[zhi, pl.ds(h * HD, HD)],
                s_out.at[h, r], r_out.at[h, r], zhi_peer(r),
            )

        return make

    def out_own(h):
        return pltpu.make_async_copy(
            out_t.at[zhi, pl.ds(h * HD, HD)], oz.at[zhi, pl.ds(h * HD, HD)], s_out.at[h, 0]
        )

    def forward_head(h):
        qkv_own(h).wait()
        for i in ((0,), (1, 2))[h]:
            each(HEADS, qkv_copy(i), "wait_recv")
        kt[h] = qkv[1, h].T
        vt[h] = qkv[2, h].T

        def body(c, carry):
            qc = qkv[0, h, rows(c, CH), :]
            t = dot(qkv[1, h], qc, 1, 1) * (scale * math.log2(math.e))
            t = jnp.concatenate([t[: SEQ - TXT], t[SEQ - TXT :] + bias_in[...]], axis=0)
            peak = jnp.max(t, axis=0, keepdims=True)
            e = jnp.exp2(t - peak)
            total = jnp.sum(e, axis=0, keepdims=True)
            pr = e * (1.0 / total)
            probs[h, c] = pr
            part = dot(vt[h], pr.astype(BF), 1, 0)
            out_t[c, pl.ds(h * HD, HD), :] = part.astype(BF)
            return carry

        lax.fori_loop(0, NCH, body, 0)
        each(4, out_copy(h), "start")
        out_own(h).start()

    def ring_step(d):
        ring_up(d - 1).wait_recv()
        if d < 4:
            ring_up(d).start()
        ring_dn(d - 1).wait_recv()
        if d < 4:
            ring_dn(d).start()

    halves = ((0, 4), (0, 2), (2, 2))

    def x_copy(i):
        first, count = halves[i]
        feats = pl.ds(min(i, 1) * HD, HD)

        def make(r):
            return remote(
                oz.at[pl.ds(first, count), feats], ox.at[x, pl.ds(first, count), feats],
                s_x.at[i, r], r_x.at[i, r], dp_peer(r),
            )

        return make

    def x_own(h):
        feats = pl.ds(h * HD, HD)
        return pltpu.make_async_copy(oz.at[:, feats], ox.at[x, :, feats], s_x.at[h, 0])

    def share_out(h):
        out_own(h).wait()
        each(4, out_copy(h), "wait_recv")
        x_own(h).start()
        for i in ((0,), (1, 2))[h]:
            each(DP, x_copy(i), "start")

    def y_copy(i):
        first, count = halves[i]
        h = min(i, 1)

        def make(r):
            dst = lax.rem(y + r, 8)
            return remote(
                wlow.at[h, pl.ds(first, count), rows(dst, 16)], yrecv.at[h, r, pl.ds(first, count)],
                s_y.at[i, r], r_y.at[i, r], y_peer(r),
            )

        return make

    def weight(i):
        first, count = halves[i]
        h = min(i, 1)
        if i < 2:
            x_own(h).wait()
        each(DP, x_copy(i), "wait_recv")

        def body(z, carry):
            total = jnp.zeros((HD, COLS), F32)
            for k in range(DP):
                part = dot(ox[k, z, pl.ds(h * HD, HD), :], nx[k], 1, 0)
                total = total + part * fbuf[k][0:1, 0:1]
            wlow[h, z] = total.astype(BF)
            return carry

        lax.fori_loop(first, first + count, body, 0)
        each(8, y_copy(i), "start")

    def d_copy(h):
        feats = pl.ds(h * HD, HD)

        def make(r):
            return remote(
                dout_s.at[r, feats], dout_t.at[zhi, feats], s_d.at[h, r], r_d.at[h, r], zhi_peer(r)
            )

        return make

    def d_own(h):
        feats = pl.ds(h * HD, HD)
        return pltpu.make_async_copy(dout_s.at[0, feats], dout_t.at[zhi, feats], s_d.at[h, 0])

    def f_copy(r):
        return remote(fbuf.at[x], fbuf.at[x], s_f.at[r], r_f.at[r], dp_peer(r))

    def make_factor():
        each(8, rew_copy, "wait_recv")
        rewards = rbuf[...].reshape(GROUP, 8, 128)
        average = jnp.sum(rewards, axis=0) / GROUP
        variance = jnp.sum((rewards - average[None]) ** 2, axis=0) / GROUP
        base = step_factor(step_sm[0], GROUP)
        fbuf[x] = base * ((rbuf[zlo, y] - average) / jnp.maximum(jnp.sqrt(variance), spread_floor))
        each(DP, f_copy, "start")

    grad_pieces = ((0, 3, 0), (0, 1, 1), (1, 1, 1), (2, 1, 1))

    def grad_copy(i):
        first, count, h = grad_pieces[i]
        cols = pl.ds(pl.multiple_of(me * FEAT + h * HD, HD), HD)

        def make(r):
            dst = lax.rem(me + r, HEADS)
            return remote(
                grads.at[pl.ds(first, count), h, rows(dst, TOK)], g_out.at[pl.ds(first, count), :, cols],
                s_o.at[i, r], r_o.at[i, r], (x, g, dst),
            )

        return make

    def grad_own(h):
        cols = pl.ds(pl.multiple_of(me * FEAT + h * HD, HD), HD)
        return pltpu.make_async_copy(grads.at[:, h, rows(me, TOK)], g_out.at[:, :, cols], s_o.at[h, 0])

    def backward_head(h):
        factor = fbuf[x][0:1, :]
        acc_k[...] = jnp.zeros_like(acc_k)
        acc_v[...] = jnp.zeros_like(acc_v)

        def body(c, carry):
            pr = probs[h, c]
            dt = dout_t[c, pl.ds(h * HD, HD), :]
            ot = out_t[c, pl.ds(h * HD, HD), :]
            row_dot = jnp.sum(dt.astype(F32) * ot.astype(F32), axis=0, keepdims=True)
            dp = dot(qkv[2, h], dt, 1, 0)
            ds = (pr * (dp - row_dot)).astype(BF)
            gqt = dot(kt[h], ds, 1, 0)
            grads[0, h, rows(c, CH), :] = (gqt.T * (scale * factor)).astype(BF)
            acc_k[...] += dot(ds, qkv[0, h, rows(c, CH), :], 1, 0)
            acc_v[...] += dot(pr.astype(BF), dt, 1, 1)
            return carry

        lax.fori_loop(0, NCH, body, 0)
        grads[1, h] = (acc_k[...] * (scale * factor)).astype(BF)
        grads[2, h] = (acc_v[...] * factor).astype(BF)
        grad_own(h).start()

    def add_y(h):
        for i in ((0,), (1, 2))[h]:
            each(8, y_copy(i), "wait_recv")
        total = wlow[h, :, rows(y, 16), :].astype(F32)
        for r in range(1, 8):
            total = total + yrecv[h, r].astype(F32)
        for z in range(4):
            zlow[2 * z + h] = total[z].astype(BF)

    def z_copy(r):
        return remote(
            zlow.at[lax.rem(2 * zhi + zlo + r, 8)], zrecv.at[r], s_z.at[r], r_z.at[r], z_peer(r)
        )

    def send_z(h):
        @pl.when(zlo == h)
        def near():
            for r in (2, 4, 6):
                z_copy(r).start()

        @pl.when(zlo != h)
        def far():
            for r in (1, 3, 5, 7):
                z_copy(r).start()

    def a_copy(r):
        part = agbuf.at[zlo, y]
        return remote(part, part, s_a.at[r], r_a.at[r], group_peer(r))

    def add_z(h):
        @pl.when(zlo == h)
        def last():
            each(8, z_copy, "wait_recv")
            part = zlow[2 * zhi + zlo].astype(F32)
            for r in range(1, 8):
                part = part + zrecv[r].astype(F32)
            agbuf[zlo, y] = part.astype(BF)
            each(GROUP, a_copy, "start")

    nx_sib.wait_recv()
    make_part(*part_groups[0])
    each(DP, part_copy(*part_groups[0], 0), "start")
    ring_step(1)
    make_part(*part_groups[1])
    each(DP, part_copy(*part_groups[1], 1), "start")
    ring_step(2)
    make_part(*part_groups[2])
    each(DP, part_copy(*part_groups[2], 2), "start")
    ring_step(3)
    forward_head(0)
    each(HEADS, qkv_copy(2), "start")
    ring_step(4)
    make_part(*part_groups[3])
    each(DP, part_copy(*part_groups[3], 3), "start")
    make_factor()
    share_out(0)
    sum_parts()
    forward_head(1)
    each(4, d_copy(0), "start")
    d_own(0).start()
    each(4, d_copy(1), "start")
    d_own(1).start()
    each(DP, f_copy, "wait_recv")
    weight(0)
    share_out(1)
    d_own(0).wait()
    each(4, d_copy(0), "wait_recv")
    backward_head(0)
    each(HEADS, grad_copy(0), "start")
    weight(1)
    weight(2)
    add_y(0)
    send_z(0)
    d_own(1).wait()
    each(4, d_copy(1), "wait_recv")
    backward_head(1)
    each(HEADS, grad_copy(1), "start")
    add_z(0)
    add_y(1)
    send_z(1)
    each(HEADS, grad_copy(2), "start")
    add_z(1)
    each(HEADS, grad_copy(3), "start")

    for h in range(2):
        each(4, out_copy(h), "wait_send")
        each(4, d_copy(h), "wait_send")
    for i in range(3):
        each(HEADS, qkv_copy(i), "wait_send")
        each(DP, x_copy(i), "wait_send")
        each(8, y_copy(i), "wait_send")
    for i, group in enumerate(part_groups):
        each(DP, part_copy(*group, i), "wait_send")
    for d in range(4):
        ring_up(d).wait_send()
        ring_dn(d).wait_send()
    each(4, p1_copy, "wait_send")
    each(DP, nx_copy, "wait_send")
    each(DP, f_copy, "wait_send")
    each(8, rew_copy, "wait_send")
    rew_first.wait_send()
    nx_sib.wait_send()

    each(GROUP, a_copy, "wait_recv")
    gp_out[...] = agbuf[...].astype(F32).reshape(FEAT, COLS)

    for h in range(2):
        grad_own(h).wait()
    for i in range(4):
        each(HEADS, grad_copy(i), "wait_recv")
        each(HEADS, grad_copy(i), "wait_send")
    each(8, z_copy, "wait_send")
    each(GROUP, a_copy, "wait_send")


def hand_out(grads, projection, gq_out, gk_out, gv_out, gp_out, sems):
    copies = [
        pltpu.make_async_copy(grads.at[a], out.at[0, 0], sems.at[a]) for a, out in enumerate((gq_out, gk_out, gv_out))
    ]
    copies.append(pltpu.make_async_copy(projection, gp_out, sems.at[3]))
    for copy in copies:
        copy.start()
    for copy in copies:
        copy.wait()


def local(queries, keys, values, noise, projection, rewards, counts, step_index):
    hbm = pl.BlockSpec(memory_space=pl.ANY)
    vmem = pl.BlockSpec(memory_space=pltpu.VMEM)
    smem = pl.BlockSpec(memory_space=pltpu.SMEM)
    dma = pltpu.SemaphoreType.DMA
    grads, grad_projection = pl.pallas_call(
        kernel,
        out_shape=(jax.ShapeDtypeStruct((3, TOK, HW), BF), jax.ShapeDtypeStruct((FEAT, COLS), F32)),
        in_specs=[hbm] * 5 + [smem] * 3,
        out_specs=(hbm, vmem),
        scratch_shapes=[
            pltpu.VMEM((3, TOK, HW), BF),
            pltpu.VMEM((3, 2, SEQ, HD), BF),
            pltpu.VMEM((DP, 2 * TOK, COLS), BF),
            pltpu.VMEM((8, 32, COLS), BF),
            pltpu.VMEM((8, 3, 32, COLS), BF),
            pltpu.VMEM((TXT, CH), F32),
            pltpu.VMEM((2, 8, 8, 128), F32),
            pltpu.VMEM((DP, 8, 128), F32),
            pltpu.VMEM((2, NCH, SEQ, CH), F32),
            pltpu.VMEM((2, HD, SEQ), BF),
            pltpu.VMEM((2, HD, SEQ), BF),
            pltpu.VMEM((NCH, FEAT, CH), BF),
            pltpu.VMEM((DP, 8, HD, CH), BF),
            pltpu.VMEM((8, HD, CH), F32),
            pltpu.VMEM((DP, 8, HD, CH), BF),
            pltpu.VMEM((NCH, FEAT, CH), BF),
            pltpu.VMEM((NCH, FEAT, CH), BF),
            pltpu.VMEM((NCH, FEAT, CH), BF),
            pltpu.VMEM((DP, NCH, FEAT, CH), BF),
            pltpu.VMEM((2, 4, HD, COLS), BF),
            pltpu.VMEM((2, 8, 4, 16, COLS), BF),
            pltpu.VMEM((8, 16, COLS), BF),
            pltpu.VMEM((8, 16, COLS), BF),
            pltpu.VMEM((2, 8, 16, COLS), BF),
            pltpu.VMEM((3, 2, SEQ, HD), BF),
            pltpu.VMEM((SEQ, HD), F32),
            pltpu.VMEM((SEQ, HD), F32),
            dma((5,)),
            dma((3, HEADS)), dma((3, HEADS)),
            dma((DP,)), dma((DP,)),
            dma((1,)), dma((1,)),
            dma((4,)), dma((4,)),
            dma((4,)), dma((4,)),
            dma((4,)), dma((4,)),
            dma((4, DP)), dma((4, DP)),
            dma((8,)), dma((8,)),
            dma((DP,)), dma((DP,)),
            dma((2, 4)), dma((2, 4)),
            dma((2, 4)), dma((2, 4)),
            dma((3, DP)), dma((3, DP)),
            dma((3, 8)), dma((3, 8)),
            dma((8,)), dma((8,)),
            dma((GROUP,)), dma((GROUP,)),
            dma((4, HEADS)), dma((4, HEADS)),
        ],
        compiler_params=pltpu.CompilerParams(
            collective_id=0, has_side_effects=True, vmem_limit_bytes=58 << 20
        ),
        name="rollout_grads",
    )(queries, keys, values, noise, projection.reshape(8, 32, COLS), rewards, counts, step_index)
    grad = jax.ShapeDtypeStruct((1, 1, TOK, HW), BF)
    return pl.pallas_call(
        hand_out,
        out_shape=(grad, grad, grad, jax.ShapeDtypeStruct((FEAT, COLS), F32)),
        in_specs=[hbm] * 2,
        out_specs=(hbm,) * 4,
        scratch_shapes=[dma((4,))],
        name="hand_out",
    )(grads, grad_projection)


def solution(mesh):
    in_specs = (
        P("dp", "group", "head", None),
        P("dp", "group", "head", None),
        P("dp", "group", "head", None),
        P("dp", "group", "head", None),
        P("head", "dp"),
        P("dp", "group"),
        P("dp"),
        P(),
    )
    out_specs = (
        P("dp", "group", "head", None),
        P("dp", "group", "head", None),
        P("dp", "group", "head", None),
        P("head", "dp"),
    )
    return jax.shard_map(local, mesh=mesh, in_specs=in_specs, out_specs=out_specs, check_vma=False)
```
